128 devices in a mesh: ctx: 32 (over x_lo, z, y), tp: 4 (over x_hi, core).
Axes of the slice: x: 4 (x_hi: 2, x_lo: 2; x = x_hi * 2 + x_lo), y: 4, z: 4, core: 2. Of those that a mesh axis runs over, the one named last changes fastest.
Arguments:
- stream_one: bfloat16 [12288, 8192], P('ctx', 'tp'), may hold values from -6 to 6
- stream_two: bfloat16 [12288, 8192], P('ctx', 'tp'), may hold values from -6 to 6
- stream_value: bfloat16 [12288, 8192], P('ctx', 'tp'), may hold values from -6 to 6
- short_stream_taps: bfloat16 [3, 7, 8192], P(None, None, 'tp'), may hold values from -6 to 6
- medium_filter: bfloat16 [512, 128], P('tp'), may hold values from -1.25 to 1.25
- residual: bfloat16 [12288, 8192], P('ctx', 'tp'), may hold values from -60 to 60
- norm_gain: bfloat16 [8192], P('tp'), may hold values from 0.5 to 1.5
- queries: bfloat16 [12288, 4096], P('ctx', 'tp'), may hold values from -12 to 12
- keys: bfloat16 [12288, 512], P('ctx', 'tp'), may hold values from -6 to 6
- values: bfloat16 [12288, 512], P('ctx', 'tp'), may hold values from -6 to 6
Outputs:
- normed: bfloat16 [12288, 8192], P('ctx', 'tp')
- attended: bfloat16 [12288, 4096], P('ctx', 'tp')
The draws below stay inside these ranges and needn't reach their ends.
All inputs are finite; a program needn't handle non-finite values.
Results may differ from the reference program's by a relative error of at most 0.0065.
Values may be sent and summed in bfloat16 or wider, within the bound.
No kernel may reach another device: no remote copies, remote signals or barrier semaphores. Data moves between devices by JAX's collectives and lax.ppermute only.
A program may use at most 128 MiB of HBM per device.

```python
import math
import jax
import jax.numpy as jnp
from jax import lax

D = 8192
GROUP = 16
SHORT = 7
MEDIUM_TAPS = 128
QH = 32
KVH = 4
HD = 128
SEQ = 12288


def draw_queries(key, part):
    key = jax.random.fold_in(key, 11)
    return jnp.clip(jax.random.normal(key, (SEQ, QH * HD), jnp.float32), -6.0, 6.0).astype(jnp.bfloat16)


def draw_keys(key, part):
    key = jax.random.fold_in(key, 13)
    return jnp.clip(jax.random.normal(key, (SEQ, KVH * HD), jnp.float32), -6.0, 6.0).astype(jnp.bfloat16)


def draw_residual(key, part):
    key = jax.random.fold_in(key, 5)
    first, second = jax.random.split(key)
    columns = jnp.arange(D, dtype=jnp.float32) / D
    row_scale = 10.0 ** jax.random.uniform(second, (SEQ, 1), jnp.float32)
    column_scale = 0.3 * 10.0 ** columns
    noise = jnp.clip(jax.random.normal(first, (SEQ, D), jnp.float32), -6.0, 6.0)
    return (noise * column_scale[None, :] * row_scale * 0.3).astype(jnp.bfloat16)


def levels(stream_key, dims, pieces, least, top_value):
    loudness = 1.0
    for axis_at, blocks in pieces:
        heights = jax.random.uniform(jax.random.fold_in(jax.random.fold_in(stream_key, 6), axis_at), (blocks,), jnp.float32, least / len(pieces), top_value / len(pieces))
        loudness = loudness * jnp.repeat(jnp.exp(heights), dims[axis_at] // blocks).reshape((-1,) + (1,) * (len(dims) - 1 - axis_at))
    return loudness


def normal_values(own_key, extent, deviation, most, cuts=(), held_as=jnp.bfloat16):
    values = jax.random.normal(own_key, extent, jnp.float32) * deviation
    if len(cuts) > 0:
        values = levels(own_key, extent, cuts, -0.22, 0.18) * values
    return jnp.clip(values, min=-most, max=most).astype(held_as)


def setup_inputs(seed: int = 0) -> dict:
    key_list = jax.random.split(jax.random.key(seed), 11)
    return {
        "stream_one": normal_values(key_list[0], (SEQ, D), 1.0, 6.0, ((0, 32), (1, 4))),
        "stream_two": normal_values(key_list[1], (SEQ, D), 1.0, 6.0, ((0, 32), (1, 4))),
        "stream_value": normal_values(key_list[2], (SEQ, D), 1.0, 6.0, ((0, 32), (1, 4))),
        "short_stream_taps": normal_values(key_list[3], (3, SHORT, D), 0.378, 6.0, ((2, 4),)),
        "medium_filter": normal_values(key_list[4], (D // GROUP, MEDIUM_TAPS), 0.0884, 1.25, ((0, 4),)),
        "residual": draw_residual(jax.random.fold_in(key_list[10], 71), 0),
        "norm_gain": jnp.clip(1.0 + 0.1 * jax.random.normal(key_list[6], (D,), jnp.float32), 0.5, 1.5).astype(jnp.bfloat16),
        "queries": draw_queries(jax.random.fold_in(key_list[10], 71), 0),
        "keys": draw_keys(jax.random.fold_in(key_list[10], 71), 0),
        "values": normal_values(key_list[9], (SEQ, KVH * HD), 1.0, 6.0, ((0, 32), (1, 4))),
    }


def causal_taps(stream, taps):
    count = taps.shape[0]
    length = stream.shape[0]
    padded = jnp.pad(stream, ((count - 1, 0), (0, 0)))
    total = jnp.zeros(stream.shape, jnp.float32)
    for j in range(count):
        total = total + taps[j].astype(jnp.float32)[None, :] * padded[count - 1 - j:count - 1 - j + length].astype(jnp.float32)
    return total

def medium_conv(mixed_in, filters):
    length, width = mixed_in.shape
    groups = filters.shape[0]
    block = MEDIUM_TAPS // 2
    span = block + MEDIUM_TAPS - 1
    filter_tap_index = jnp.arange(block, dtype=jnp.int32)[:, None] + (MEDIUM_TAPS - 1) - jnp.arange(span, dtype=jnp.int32)[None, :]
    valid = (filter_tap_index >= 0) & (filter_tap_index < MEDIUM_TAPS)
    picked = filters.astype(jnp.float32)[:, jnp.clip(filter_tap_index, 0, MEDIUM_TAPS - 1)]
    toeplitz = jnp.where(valid[None], picked, 0.0)
    padded = jnp.pad(mixed_in, ((MEDIUM_TAPS - 1, 0), (0, 0)))

    def one_block(start):
        piece = lax.dynamic_slice_in_dim(padded, start, span, 0).astype(jnp.float32).reshape(span, groups, GROUP)
        return jnp.einsum('gts,sgc->tgc', toeplitz, piece).reshape(block, width)
    starts = jnp.arange(length // block, dtype=jnp.int32) * block
    return lax.map(one_block, starts).reshape(length, width)

def attend(queries, keys, values):
    length = queries.shape[0]
    ratio = QH // KVH
    scale = 1.0 / math.sqrt(HD)
    q_all = queries.reshape(length, KVH, ratio, HD)
    k_all = keys.reshape(length, KVH, HD)
    v_all = values.reshape(length, KVH, HD)
    size = 256
    blocks = length // size
    key_pos = jnp.arange(length, dtype=jnp.int32)

    def one_item(item):
        group = item // blocks
        start = item % blocks * size
        q_block = lax.dynamic_slice_in_dim(q_all, start, size, 0)
        q_block = lax.dynamic_index_in_dim(q_block, group, 1, keepdims=False).astype(jnp.float32)
        k_group = lax.dynamic_index_in_dim(k_all, group, 1, keepdims=False).astype(jnp.float32)
        value_group = lax.dynamic_index_in_dim(v_all, group, 1, keepdims=False).astype(jnp.float32)
        scores = jnp.einsum('brd,sd->rbs', q_block, k_group) * scale
        query_pos = start + jnp.arange(size, dtype=jnp.int32)
        allowed = key_pos[None, :] <= query_pos[:, None]
        scores = jnp.where(allowed[None], scores, -jnp.inf)
        top = lax.optimization_barrier(jnp.max(scores, axis=-1, keepdims=True))
        probs = jnp.exp(scores - top)
        totals = lax.optimization_barrier(jnp.sum(probs, axis=-1))
        weights = lax.optimization_barrier(probs.astype(jnp.bfloat16)).astype(jnp.float32)
        result = jnp.einsum('rbs,sd->rbd', weights, value_group) / totals[..., None]
        return result.astype(jnp.bfloat16)
    results = lax.map(one_item, jnp.arange(KVH * blocks, dtype=jnp.int32))
    results = results.reshape(KVH, blocks, ratio, size, HD).transpose(1, 3, 0, 2, 4)
    return results.reshape(length, QH * HD)

def reference(stream_one, stream_two, stream_value, short_stream_taps, medium_filter, residual, norm_gain, queries, keys, values):
    first_short = causal_taps(stream_one, short_stream_taps[0])
    value_short = causal_taps(stream_value, short_stream_taps[2])
    mixed_in = lax.optimization_barrier((first_short * value_short).astype(jnp.bfloat16))
    medium = medium_conv(mixed_in, medium_filter)
    gate_short = causal_taps(stream_two, short_stream_taps[1])
    branch_sum = residual.astype(jnp.float32) + gate_short * medium
    mean_square = lax.optimization_barrier(jnp.mean(branch_sum * branch_sum, axis=1, keepdims=True))
    normed = (branch_sum * lax.rsqrt(mean_square + 1e-06) * norm_gain.astype(jnp.float32)[None, :]).astype(jnp.bfloat16)
    attended = attend(queries, keys, values)
    return (normed, attended)
```

```python
import functools
import math

import jax
import jax.numpy as jnp
import numpy as np
from jax import lax
from jax.experimental import pallas as pl
from jax.experimental.pallas import tpu as pltpu
from jax.sharding import PartitionSpec as P

f32=jnp.float32; bf=jnp.bfloat16
SHORT=7; GROUP=16; LANES=128; EDGE=16; TAPS=128; BLK=64

def tail_kernel(one, two, val, taps, out, x_scr):
    keep = TAPS
    last = one.shape[0]
    t = taps[...].astype(f32)
    def short(ref, which, slot):
        x_scr[slot] = ref[last - keep - EDGE:, :].astype(f32)
        total = t[which, 0:1] * x_scr[slot, EDGE:EDGE + keep, :]
        for j in range(1, SHORT):
            total += t[which, j:j + 1] * x_scr[slot, EDGE - j:EDGE - j + keep, :]
        return total
    out[0:keep] = (short(one, 0, 0) * short(val, 2, 1)).astype(bf)
    for n, ref in enumerate((one, two, val)):
        out[keep + EDGE * n:keep + EDGE * (n + 1)] = ref[last - EDGE:, :]

def tail_call(one, two, val, taps):
    rows, width = one.shape
    spec = pl.BlockSpec((rows, LANES), lambda i: (0, i))
    out_rows = TAPS + 3 * EDGE
    return pl.pallas_call(tail_kernel, grid=(width // LANES,),
        in_specs=[spec] * 3 + [pl.BlockSpec((3, SHORT, LANES), lambda i: (0, 0, i))],
        out_specs=pl.BlockSpec((out_rows, LANES), lambda i: (0, i)),
        out_shape=jax.ShapeDtypeStruct((out_rows, width), bf),
        scratch_shapes=[pltpu.VMEM((2, TAPS + EDGE, LANES), f32)],
        name="mixed_tail")(one, two, val, taps)

def mixer_kernel(one, two, val, halo, taps, rev, res, branch, squares, x_scr, m_scr, t_scr):
    rows = one.shape[0]
    t = taps[...].astype(f32)
    def short(ref, n):
        lo = TAPS + EDGE * n
        x_scr[n, 0:EDGE] = halo[lo:lo + EDGE, :].astype(f32)
        x_scr[n, EDGE:] = ref[...].astype(f32)
        total = t[n, 0:1] * x_scr[n, EDGE:, :]
        for j in range(1, SHORT):
            total += t[n, j:j + 1] * x_scr[n, EDGE - j:EDGE - j + rows, :]
        return total
    m_scr[0:TAPS] = halo[0:TAPS]
    m_scr[TAPS:] = (short(one, 0) * short(val, 2)).astype(bf)
    gate = short(two, 1)
    groups = LANES // GROUP
    for g in range(groups):
        row = jnp.broadcast_to(rev[g:g + 1, :], (BLK, 2 * TAPS))
        rolled = pltpu.roll(row, 0, 1, stride=1, stride_axis=0)
        t_scr[g * BLK:(g + 1) * BLK] = rolled.astype(bf)
    lane = lax.broadcasted_iota(jnp.int32, (BLK, LANES), 1) // GROUP
    span = BLK + TAPS
    total = jnp.zeros((8, 128), f32)
    for pair in range(rows // (2 * BLK)):
        at = 2 * BLK * pair
        window = jnp.concatenate([m_scr[at:at + span], m_scr[at + BLK:at + BLK + span]], axis=1)
        wide = jnp.dot(t_scr[:, :span], window, preferred_element_type=f32)
        for half in range(2):
            r = slice(at + BLK * half, at + BLK * (half + 1))
            c = slice(LANES * half, LANES * (half + 1))
            medium = wide[0:BLK, c]
            for g in range(1, groups):
                medium = jnp.where(lane == g, wide[g * BLK:(g + 1) * BLK, c], medium)
            summed = res[r].astype(f32) + gate[r] * medium
            branch[r] = summed
            sq = summed * summed
            @pl.when(pl.program_id(0) == 0)
            def _(): squares[r] = sq
            @pl.when(pl.program_id(0) > 0)
            def _(): squares[r] += sq

def mixer_call(one, two, val, halo, taps, rev, res):
    rows, width = one.shape
    spec = pl.BlockSpec((rows, LANES), lambda i: (0, i))
    groups = LANES // GROUP
    return pl.pallas_call(mixer_kernel, grid=(width // LANES,),
        in_specs=[spec] * 3 + [pl.BlockSpec((halo.shape[0], LANES), lambda i: (0, i)),
            pl.BlockSpec((3, SHORT, LANES), lambda i: (0, 0, i)),
            pl.BlockSpec((groups, 2 * TAPS), lambda i: (i, 0)), spec],
        out_specs=[spec, pl.BlockSpec((rows, LANES), lambda i: (0, 0))],
        out_shape=[jax.ShapeDtypeStruct((rows, width), f32), jax.ShapeDtypeStruct((rows, LANES), f32)],
        scratch_shapes=[pltpu.VMEM((3, EDGE + rows, LANES), f32), pltpu.VMEM((TAPS + rows, LANES), bf),
            pltpu.VMEM((groups * BLK, 2 * TAPS), bf)],
        compiler_params=pltpu.CompilerParams(vmem_limit_bytes=32 * 2**20),
        name="mixer")(one, two, val, halo, taps, rev, res)

def reversed_taps(filters):
    flipped = filters.astype(f32)[:, ::-1]
    return jnp.pad(flipped, ((0, 0), (1, TAPS - 1)))


HD = 128
PAIR = 2
ONES = 16
EMPTY, FULL, DIAGONAL = 0, 1, 2
SCALE = math.log2(math.e) / math.sqrt(HD)


def pack_kernel(keys, values, packed):
    packed[:, :HD] = keys[...]
    turned = values[...].astype(f32).T.astype(bf)
    for part in range(values.shape[0] // HD):
        packed[part * HD:(part + 1) * HD, HD:] = turned[:, part * HD:(part + 1) * HD]


def pack_call(keys, values):
    return pl.pallas_call(pack_kernel, out_shape=jax.ShapeDtypeStruct((keys.shape[0], 2 * HD), bf),
                          name="pack_keys")(keys, values)


def turn_kernel(queries, turned):
    rows = queries.shape[0]
    for head in range(PAIR):
        wide = queries[:, head * HD:(head + 1) * HD].astype(f32).T * SCALE
        high = wide.astype(bf)
        columns = slice(head * rows, (head + 1) * rows)
        turned[0, :HD, columns] = high
        turned[0, HD:, columns] = (wide - high.astype(f32)).astype(bf)


def turn_call(queries):
    rows, width = queries.shape
    pairs = width // (PAIR * HD)
    return pl.pallas_call(turn_kernel, grid=(pairs,),
        in_specs=[pl.BlockSpec((rows, PAIR * HD), lambda i: (0, i))],
        out_specs=pl.BlockSpec((1, 2 * HD, PAIR * rows), lambda i: (i, 0, 0)),
        out_shape=jax.ShapeDtypeStruct((pairs, 2 * HD, PAIR * rows), bf),
        name="turn_queries")(queries)


def attend_kernel(first, last, sizes, pairs, rows, *refs):
    refs = list(refs)
    table, q_hbm = refs[0], refs[1]
    at = 2
    pieces = refs[at:at + len(sizes)]
    at += len(sizes)
    if not first:
        acc_in, top_in = refs[at:at + 2]
        at += 2
    if last:
        out = refs[at]
        at += 1
    else:
        acc_out, top_out = refs[at:at + 2]
        at += 2
    q, kv, acc, top, scores, probs, factors, load_sem, kv_sem, store_sem = refs[at:]
    shards = sum(sizes)
    me = lax.axis_index("ctx")
    count = table[me, 0]

    def kv_copies():
        number = 0
        for piece, size in zip(pieces, sizes):
            for index in range(size):
                slot = table[me, 1 + number]
                yield slot, pltpu.make_async_copy(piece.at[index], kv.at[jnp.maximum(slot, 0)], kv_sem.at[number])
                number += 1

    for slot, copy in kv_copies():
        pl.when(slot >= 0)(copy.start)
    loads = [pltpu.make_async_copy(q_hbm, q, load_sem.at[0])]
    if not first:
        loads.append(pltpu.make_async_copy(acc_in, acc, load_sem.at[1]))
        loads.append(pltpu.make_async_copy(top_in, top, load_sem.at[2]))
    for copy in loads:
        copy.start()
    blocks = kv.shape[0] // 2

    if first:
        acc[...] = jnp.zeros_like(acc)
        top[...] = jnp.full_like(top, -1e30)
    if shards % 2 or True:
        for block in range(blocks):
            @pl.when(table[me, 1 + shards] == block)
            def _():
                kv[2 * block + 1] = jnp.zeros(kv.shape[1:], kv.dtype)
    for slot, copy in kv_copies():
        pl.when(slot >= 0)(copy.wait)
    for copy in loads:
        copy.wait()

    def entry(number):
        code = table[me, 2 + shards + jnp.minimum(number, count - 1)]
        return code % 8, (code // 8) % 16, (code // 128) % 2, (code // 256) % 4, (code // 1024) % 4

    def multiply_keys(number, slot):
        pair, block = entry(number)[:2]
        k = jnp.concatenate([kv[2 * block, :, :HD], kv[2 * block + 1, :, :HD]], axis=0)
        k = jnp.concatenate([k, k], axis=1)
        scores[slot] = jnp.dot(k, q[pair], preferred_element_type=f32)

    def multiply_values(number, slot):
        pair, block = entry(number)[:2]
        parts = rows // HD
        v = jnp.concatenate([kv[2 * block + n // parts, (n % parts) * HD:(n % parts + 1) * HD, HD:]
                             for n in range(2 * parts)], axis=1)
        v = jnp.concatenate([v, jnp.ones((ONES, 2 * rows), bf)], axis=0)
        product = jnp.dot(v, probs[slot], preferred_element_type=f32)
        acc[pair] = acc[pair] * factors[slot, 0:1] + product

    def mask(number, slot):
        _, _, masked, mode0, mode1 = entry(number)

        @pl.when(masked == 1)
        def _():
            key = lax.broadcasted_iota(jnp.int32, (rows, rows), 0)
            query = lax.broadcasted_iota(jnp.int32, (rows, rows), 1)
            for half, mode in enumerate((mode0, mode1)):
                limit = jnp.where(mode == FULL, rows, jnp.where(mode == DIAGONAL, 0, -2 * rows))
                allowed = key - query <= limit
                for head in range(PAIR):
                    r = slice(half * rows, (half + 1) * rows)
                    c = slice(head * rows, (head + 1) * rows)
                    scores[slot, r, c] = jnp.where(allowed, scores[slot, r, c], -1e30)

    def half_step(number, slot):
        mask(number, slot)
        multiply_keys(number + 1, 1 - slot)
        multiply_values(jnp.maximum(number - 1, 0), 1 - slot)
        pair = entry(number)[0]
        s = scores[slot]
        old = top[pair, 0:1]
        new = jnp.maximum(old, jnp.max(s, axis=0, keepdims=True))
        factors[slot, 0:1] = jnp.exp2(old - new)
        top[pair, 0:1] = new
        probs[slot] = jnp.exp2(s - new).astype(bf)

    @pl.when(count > 0)
    def _():
        probs[1] = jnp.zeros(probs.shape[1:], bf)
        factors[1] = jnp.ones(factors.shape[1:], f32)
        multiply_keys(0, 0)

        @pl.loop(0, (count + 1) // 2)
        def _(step):
            half_step(2 * step, 0)
            @pl.when(2 * step + 1 < count)
            def _():
                half_step(2 * step + 1, 1)

        for parity in range(2):
            @pl.when((count - 1) % 2 == parity)
            def _():
                multiply_values(count - 1, parity)

    if last:
        for pair in range(pairs):
            for head in range(PAIR):
                c = slice(head * rows, (head + 1) * rows)
                value = acc[pair, :HD, c] / acc[pair, HD:HD + 1, c]
                at = (pair * PAIR + head) * HD
                out[:, at:at + HD] = value.T.astype(bf)
    else:
        stores = [pltpu.make_async_copy(acc, acc_out, store_sem.at[0]), pltpu.make_async_copy(top, top_out, store_sem.at[1])]
        for copy in stores:
            copy.start()
        for copy in stores:
            copy.wait()


def attend_call(table, turned, pieces, state, last, entries):
    pairs, _, wide = turned.shape
    rows = wide // PAIR
    sizes = tuple(piece.shape[0] for piece in pieces)
    shards = sum(sizes)
    slots = shards + shards % 2
    first = state is None
    acc_shape = jax.ShapeDtypeStruct((pairs, HD + ONES, wide), f32)
    top_shape = jax.ShapeDtypeStruct((pairs, 8, wide), f32)
    hbm = pl.BlockSpec(memory_space=pl.ANY)
    operands = [table, turned, *pieces] + ([] if first else list(state))
    if last:
        out_shape = jax.ShapeDtypeStruct((rows, pairs * PAIR * HD), bf)
        out_specs = pl.BlockSpec(memory_space=pltpu.VMEM)
    else:
        out_shape = [acc_shape, top_shape]
        out_specs = [hbm, hbm]
    return pl.pallas_call(
        functools.partial(attend_kernel, first, last, sizes, pairs, rows),
        in_specs=[pl.BlockSpec(memory_space=pltpu.SMEM)] + [hbm] * (len(operands) - 1),
        out_specs=out_specs,
        out_shape=out_shape,
        scratch_shapes=[
            pltpu.VMEM(turned.shape, bf),
            pltpu.VMEM((slots, rows, 2 * HD), bf),
            pltpu.VMEM(acc_shape.shape, f32),
            pltpu.VMEM(top_shape.shape, f32),
            pltpu.VMEM((2, 2 * rows, wide), f32),
            pltpu.VMEM((2, 2 * rows, wide), bf),
            pltpu.VMEM((2, 8, wide), f32),
            pltpu.SemaphoreType.DMA((3,)),
            pltpu.SemaphoreType.DMA((shards,)),
            pltpu.SemaphoreType.DMA((2,)),
        ],
        compiler_params=pltpu.CompilerParams(vmem_limit_bytes=48 * 2**20),
        cost_estimate=pl.CostEstimate(flops=entries * 8 * rows * rows * 4 * HD, bytes_accessed=4 * 2**20, transcendentals=0),
        name="attend",
    )(*operands)


def make_table(sources_of, pairs, offset=0):
    rows_out = []
    for me, sources in enumerate(sources_of):
        shards = len(sources)
        allowed = [n for n, source in enumerate(sources) if source <= me]
        slot = {n: at for at, n in enumerate(allowed)}
        modes = [DIAGONAL if sources[n] == me else FULL for n in allowed]
        odd = len(modes) % 2
        modes = modes + [EMPTY] * odd
        codes = []
        for block in range(len(modes) // 2):
            pair_modes = modes[2 * block:2 * block + 2]
            masked = int(pair_modes != [FULL, FULL])
            for pair in range(pairs):
                codes.append(pair + 8 * block + 128 * masked + 256 * pair_modes[0] + 1024 * pair_modes[1])
        most = pairs * ((shards + 1) // 2)
        line = [len(codes)] + [slot.get(n, -1) for n in range(shards)] + [len(modes) // 2 - 1 if odd else -1]
        rows_out.append(line + codes + [0] * (most - len(codes)))
    return np.array(rows_out, np.int32)


D = 8192
Z = Y = 4
PLANE = Z * Y


def split(i):
    return i // PLANE, (i // Y) % Z, i % Y


def neighbour(i, x=0, z=0, y=0):
    at_x, at_z, at_y = split(i)
    return (at_x + x) % 2 * PLANE + (at_z + z) % Z * Y + (at_y + y) % Y


def moved(value, x=0, z=0, y=0):
    pairs = [(i, neighbour(i, x, z, y)) for i in range(2 * PLANE)]
    return lax.ppermute(value, "ctx", pairs)


def gathered(first, axis, other):
    near = [first] + [moved(first, **{axis: step}) for step in (1, -1, 2)]
    line = jnp.stack(near)
    behind = moved(line, **{other: 1})
    ahead = moved(line, **{other: -1})
    half = line.shape[0] // 2
    low = moved(behind[:half], **{other: 1})
    high = moved(ahead[half:], **{other: -1})
    return near[1:], [behind, ahead], [low, high]


def sources_of(me, plane, axis, other):
    base = plane * PLANE + me % PLANE
    line = [neighbour(base, **{axis: -step}) for step in (0, 1, -1, 2)]
    def shifted(blocks, step):
        return [neighbour(b, **{other: -step}) for b in blocks]
    return line[1:], shifted(line, 1) + shifted(line, -1), shifted(line[:2], 2) + shifted(line[2:], -2)


def tables(pairs):
    everyone = range(2 * PLANE)
    chunks = [[[me, neighbour(me, x=1)] for me in everyone]]
    for stage in range(3):
        chunks.append([sources_of(me, 0, "z", "y")[stage] + sources_of(me, 1, "y", "z")[stage] for me in everyone])
    for me in everyone:
        assert sorted(sum((c[me] for c in chunks), [])) == list(everyone)
    return [make_table(c, pairs) for c in chunks]


def shards(stream_one, stream_two, stream_value, short_stream_taps, medium_filter, residual, norm_gain, queries, keys, values):
    rows, width = stream_one.shape
    pairs = queries.shape[1] // (PAIR * HD)
    own = pack_call(keys, values)
    other = moved(own, x=1)
    tail = tail_call(stream_one, stream_two, stream_value, short_stream_taps)
    halo = lax.ppermute(tail, "ctx", [(i, i + 1) for i in range(2 * PLANE - 1)])
    turned = turn_call(queries)
    low = lax.axis_index("ctx") < PLANE
    first = jnp.where(low, own, other)
    second = jnp.where(low, other, own)
    a = gathered(first, "z", "y")
    b = gathered(second, "y", "z")
    lists = tables(pairs)
    state = attend_call(lists[0], turned, [own[None], other[None]], None, False, pairs)
    state = attend_call(lists[1], turned, [p[None] for p in a[0] + b[0]], state, False, 3 * pairs)
    branch, squares = mixer_call(stream_one, stream_two, stream_value, halo, short_stream_taps, reversed_taps(medium_filter), residual)
    state = attend_call(lists[2], turned, a[1] + b[1], state, False, 8 * pairs)
    attended = attend_call(lists[3], turned, a[2] + b[2], state, True, 4 * pairs)
    total = lax.psum(jnp.sum(squares, axis=1), "tp")
    scaling = lax.rsqrt(total / D + 1e-06)
    normed = (branch * scaling[:, None] * norm_gain.astype(f32)[None, :]).astype(bf)
    return normed, attended


def solution(mesh):
    in_specs = (P("ctx", "tp"), P("ctx", "tp"), P("ctx", "tp"), P(None, None, "tp"), P("tp", None),
                P("ctx", "tp"), P("tp"), P("ctx", "tp"), P("ctx", "tp"), P("ctx", "tp"))
    return jax.shard_map(shards, mesh=mesh, in_specs=in_specs, out_specs=(P("ctx", "tp"), P("ctx", "tp")), check_vma=False)
```

```python
import functools
import math

import jax
import jax.numpy as jnp
import numpy as np
from jax import lax
from jax.experimental import pallas as pl
from jax.experimental.pallas import tpu as pltpu
from jax.sharding import PartitionSpec as P

f32=jnp.float32; bf=jnp.bfloat16
SHORT=7; GROUP=16; LANES=128; EDGE=16; TAPS=128; BLK=64

def tail_kernel(one, two, val, taps, out, x_scr):
    keep = TAPS
    last = one.shape[0]
    for lanes in range(one.shape[1] // LANES):
        c = slice(lanes * LANES, (lanes + 1) * LANES)
        t = taps[:, :, c].astype(f32)

        def short(ref, which, slot):
            x_scr[slot] = ref[last - keep - EDGE:, c].astype(f32)
            total = t[which, 0:1] * x_scr[slot, EDGE:EDGE + keep, :]
            for j in range(1, SHORT):
                total += t[which, j:j + 1] * x_scr[slot, EDGE - j:EDGE - j + keep, :]
            return total
        out[0:keep, c] = (short(one, 0, 2 * (lanes % 2)) * short(val, 2, 2 * (lanes % 2) + 1)).astype(bf)
    for n, ref in enumerate((one, two, val)):
        out[keep + EDGE * n:keep + EDGE * (n + 1)] = ref[last - EDGE:, :]


def tail_call(one, two, val, taps):
    rows, width = one.shape
    tile = 4 * LANES
    spec = pl.BlockSpec((rows // 2, tile), lambda i: (1, i))
    out_rows = TAPS + 3 * EDGE
    return pl.pallas_call(tail_kernel, grid=(width // tile,),
        in_specs=[spec] * 3 + [pl.BlockSpec((3, SHORT, tile), lambda i: (0, 0, i))],
        out_specs=pl.BlockSpec((out_rows, tile), lambda i: (0, i)),
        out_shape=jax.ShapeDtypeStruct((out_rows, width), bf),
        scratch_shapes=[pltpu.VMEM((4, TAPS + EDGE, LANES), f32)],
        name="mixed_tail")(one, two, val, taps)


def mixer_kernel(one, two, val, halo, taps, rev, res, branch, squares, x_scr, m_scr, t_scr):
    rows = one.shape[0]
    t = taps[...].astype(f32)
    def short(ref, n):
        lo = TAPS + EDGE * n
        x_scr[n, 0:EDGE] = halo[lo:lo + EDGE, :].astype(f32)
        x_scr[n, EDGE:] = ref[...].astype(f32)
        total = t[n, 0:1] * x_scr[n, EDGE:, :]
        for j in range(1, SHORT):
            total += t[n, j:j + 1] * x_scr[n, EDGE - j:EDGE - j + rows, :]
        return total
    m_scr[0:TAPS] = halo[0:TAPS]
    m_scr[TAPS:] = (short(one, 0) * short(val, 2)).astype(bf)
    gate = short(two, 1)
    groups = LANES // GROUP
    for g in range(groups):
        row = jnp.broadcast_to(rev[g:g + 1, :], (BLK, 2 * TAPS))
        rolled = pltpu.roll(row, 0, 1, stride=1, stride_axis=0)
        t_scr[g * BLK:(g + 1) * BLK] = rolled.astype(bf)
    lane = lax.broadcasted_iota(jnp.int32, (BLK, LANES), 1) // GROUP
    span = BLK + TAPS
    total = jnp.zeros((8, 128), f32)
    for pair in range(rows // (2 * BLK)):
        at = 2 * BLK * pair
        window = jnp.concatenate([m_scr[at:at + span], m_scr[at + BLK:at + BLK + span]], axis=1)
        wide = jnp.dot(t_scr[:, :span], window, preferred_element_type=f32)
        for half in range(2):
            r = slice(at + BLK * half, at + BLK * (half + 1))
            c = slice(LANES * half, LANES * (half + 1))
            medium = wide[0:BLK, c]
            for g in range(1, groups):
                medium = jnp.where(lane == g, wide[g * BLK:(g + 1) * BLK, c], medium)
            summed = res[r].astype(f32) + gate[r] * medium
            branch[r] = summed
            sq = summed * summed
            @pl.when(pl.program_id(0) == 0)
            def _(): squares[r] = sq
            @pl.when(pl.program_id(0) > 0)
            def _(): squares[r] += sq

def mixer_call(one, two, val, halo, taps, rev, res):
    rows, width = one.shape
    spec = pl.BlockSpec((rows, LANES), lambda i: (0, i))
    groups = LANES // GROUP
    return pl.pallas_call(mixer_kernel, grid=(width // LANES,),
        in_specs=[spec] * 3 + [pl.BlockSpec((halo.shape[0], LANES), lambda i: (0, i)),
            pl.BlockSpec((3, SHORT, LANES), lambda i: (0, 0, i)),
            pl.BlockSpec((groups, 2 * TAPS), lambda i: (i, 0)), spec],
        out_specs=[spec, pl.BlockSpec((rows, LANES), lambda i: (0, 0))],
        out_shape=[jax.ShapeDtypeStruct((rows, width), f32), jax.ShapeDtypeStruct((rows, LANES), f32)],
        scratch_shapes=[pltpu.VMEM((3, EDGE + rows, LANES), f32), pltpu.VMEM((TAPS + rows, LANES), bf),
            pltpu.VMEM((groups * BLK, 2 * TAPS), bf)],
        compiler_params=pltpu.CompilerParams(vmem_limit_bytes=32 * 2**20),
        name="mixer")(one, two, val, halo, taps, rev, res)

def reversed_taps(filters):
    flipped = filters.astype(f32)[:, ::-1]
    return jnp.pad(flipped, ((0, 0), (1, TAPS - 1)))


HD = 128
QUAD = 4
ONES = 16
EMPTY, FULL, DIAGONAL = 0, 1, 2
DUMMIES = 3
SCALE = math.log2(math.e) / math.sqrt(HD)


def pack_kernel(keys, values, packed):
    packed[:, :HD] = keys[...]
    turned = values[...].astype(f32).T.astype(bf)
    for part in range(values.shape[0] // HD):
        packed[part * HD:(part + 1) * HD, HD:] = turned[:, part * HD:(part + 1) * HD]


def pack_call(keys, values):
    return pl.pallas_call(pack_kernel, out_shape=jax.ShapeDtypeStruct((keys.shape[0], 2 * HD), bf),
                          name="pack_keys")(keys, values)


def turn_kernel(queries, turned):
    rows = queries.shape[0]
    for head in range(QUAD):
        wide = queries[:, head * HD:(head + 1) * HD].astype(f32).T * SCALE
        high = wide.astype(bf)
        columns = slice(head * rows, (head + 1) * rows)
        turned[0, :HD, columns] = high
        turned[0, HD:, columns] = (wide - high.astype(f32)).astype(bf)


def turn_call(queries):
    rows, width = queries.shape
    quads = width // (QUAD * HD)
    return pl.pallas_call(turn_kernel, grid=(quads,),
        in_specs=[pl.BlockSpec((rows, QUAD * HD), lambda i: (0, i))],
        out_specs=pl.BlockSpec((1, 2 * HD, QUAD * rows), lambda i: (i, 0, 0)),
        out_shape=jax.ShapeDtypeStruct((quads, 2 * HD, QUAD * rows), bf),
        name="turn_queries")(queries)


def table_layout(shards):
    slots = shards + DUMMIES + (shards + DUMMIES) % 2
    at_a = 2 + DUMMIES
    at_b = at_a + shards
    at_live = at_b + shards
    at_fast = at_live + slots
    at_slow = at_fast + 3 * (slots // 2)
    return slots, at_a, at_b, at_live, at_fast, at_slow, at_slow + 3 * (slots // 2)


def attend_kernel(sizes, groups, starts, last, rows, *refs):
    refs = list(refs)
    take = lambda n: [refs.pop(0) for _ in range(n)]
    table, = take(1)
    pieces = take(len(sizes))
    q_in = take(len(groups))
    state_in = [None if start else take(2) for start in starts]
    results = take(len(groups)) if last else [take(2) for _ in groups]
    q, kv, acc, top, s_scr, p_scr, a_scr, load_sem, kv_sem, store_sem = refs
    shards = sum(sizes)
    slots, at_a, at_b, at_live, at_fast, at_slow, _ = table_layout(shards)
    me = lax.axis_index("ctx")
    n_fast = table[me, 0]
    n_slow = table[me, 1]
    half = 2 * rows
    parts = rows // HD

    copies = []
    number = 0
    for piece, size in zip(pieces, sizes):
        for index in range(size):
            for n, at in enumerate((at_a, at_b)):
                slot = table[me, at + number]
                copies.append((slot, pltpu.make_async_copy(
                    piece.at[index], kv.at[jnp.maximum(slot, 0)], kv_sem.at[2 * number + n])))
            number += 1
    for slot, copy in copies:
        pl.when(slot >= 0)(copy.start)
    loads = []
    at = 0
    for n, count in enumerate(groups):
        group = pl.ds(at, count)
        loads.append(pltpu.make_async_copy(q_in[n], q.at[group], load_sem.at[3 * n]))
        if not starts[n]:
            loads.append(pltpu.make_async_copy(state_in[n][0], acc.at[group], load_sem.at[3 * n + 1]))
            loads.append(pltpu.make_async_copy(state_in[n][1], top.at[group], load_sem.at[3 * n + 2]))
        at += count
    for copy in loads:
        copy.start()
    at = 0
    for n, count in enumerate(groups):
        if starts[n]:
            for quad in range(at, at + count):
                acc[quad] = jnp.zeros(acc.shape[1:], f32)
                top[quad] = jnp.full(top.shape[1:], -1e30, f32)
        at += count
    for slot, copy in copies:
        pl.when(slot >= 0)(copy.wait)
    for copy in loads:
        copy.wait()
    for n in range(DUMMIES):
        slot = table[me, 2 + n]

        @pl.when(slot >= 0)
        def _():
            kv[slot, :, HD:] = jnp.zeros((rows, HD), bf)

    def decode(code):
        return code % 4, (code // 4) % 64, (code // 256) % 4, (code // 1024) % 4

    def columns(pair):
        return slice(pair * half, (pair + 1) * half)

    def multiply_keys(quad, block, pair):
        k = jnp.concatenate([kv[2 * block, :, :HD], kv[2 * block + 1, :, :HD]], axis=0)
        k = jnp.concatenate([k, k], axis=1)
        return jnp.dot(k, q[quad, :, columns(pair)], preferred_element_type=f32)

    def multiply_values(quad, block, pair, weights, factor):
        v = jnp.concatenate([kv[2 * block + n // parts, (n % parts) * HD:(n % parts + 1) * HD, HD:]
                             for n in range(2 * parts)], axis=1)
        live = [jnp.full((ONES, rows), table[me, at_live + 2 * block + n].astype(f32)).astype(bf) for n in range(2)]
        v = jnp.concatenate([v, jnp.concatenate(live, axis=1)], axis=0)
        c = columns(pair)
        acc[quad, :, c] = acc[quad, :, c] * factor + jnp.dot(v, weights, preferred_element_type=f32)

    def soften(quad, pair, s):
        c = columns(pair)
        old = top[quad, 0:1, c]
        new = jnp.maximum(old, jnp.max(s, axis=0, keepdims=True))
        top[quad, 0:1, c] = new
        return jnp.exp2(s - new).astype(bf), jnp.exp2(old - new)

    @pl.loop(0, n_slow)
    def _(number):
        quad, block, *modes = decode(table[me, at_slow + number])
        for pair in range(2):
            s_scr[...] = multiply_keys(quad, block, pair)
            key = lax.broadcasted_iota(jnp.int32, (rows, rows), 0)
            query = lax.broadcasted_iota(jnp.int32, (rows, rows), 1)
            for part, mode in enumerate(modes):
                limit = jnp.where(mode == FULL, rows, jnp.where(mode == DIAGONAL, 0, -2 * rows))
                allowed = key - query <= limit
                for head in range(2):
                    r = slice(part * rows, (part + 1) * rows)
                    c = slice(head * rows, (head + 1) * rows)
                    s_scr[r, c] = jnp.where(allowed, s_scr[r, c], -1e30)
            weights, factor = soften(quad, pair, s_scr[...])
            multiply_values(quad, block, pair, weights, factor)

    def fast_entry(number):
        return decode(table[me, at_fast + jnp.clip(number, 0, n_fast - 1)])[:2]

    def region(number, unroll):
        todo = [(*fast_entry(number + n), pair) for n in range(unroll) for pair in range(2)]
        todo.append((*fast_entry(number + unroll), 0))
        s = s_scr[...]
        pending = (*fast_entry(number - 1), 1, p_scr[...], a_scr[0:1])
        for now, later in zip(todo, todo[1:]):
            coming = multiply_keys(*later)
            multiply_values(*pending)
            quad, block, pair = now
            weights, factor = soften(quad, pair, s)
            pending = (quad, block, pair, weights, factor)
            s = coming
        s_scr[...] = s
        p_scr[...] = pending[3]
        a_scr[0:1] = pending[4]

    @pl.when(n_fast > 0)
    def _():
        s_scr[...] = multiply_keys(*fast_entry(0), 0)
        p_scr[...] = jnp.zeros_like(p_scr)
        a_scr[...] = jnp.ones_like(a_scr)

        @pl.loop(0, n_fast // 2)
        def _(step):
            region(2 * step, 2)

        @pl.when(n_fast % 2 == 1)
        def _():
            region(n_fast - 1, 1)

        multiply_values(*fast_entry(n_fast - 1), 1, p_scr[...], a_scr[0:1])

    if last:
        at = 0
        for n, count in enumerate(groups):
            for quad in range(count):
                for head in range(QUAD):
                    c = slice(head * rows, (head + 1) * rows)
                    value = acc[at + quad, :HD, c] / acc[at + quad, HD:HD + 1, c]
                    to = (quad * QUAD + head) * HD
                    results[n][:, to:to + HD] = value.T.astype(bf)
            at += count
    else:
        stores = []
        at = 0
        for n, count in enumerate(groups):
            group = pl.ds(at, count)
            stores.append(pltpu.make_async_copy(acc.at[group], results[n][0], store_sem.at[2 * n]))
            stores.append(pltpu.make_async_copy(top.at[group], results[n][1], store_sem.at[2 * n + 1]))
            at += count
        for copy in stores:
            copy.start()
        for copy in stores:
            copy.wait()


def attend_call(table, pieces, turned, states, last=False):
    wide = turned[0].shape[2]
    rows = wide // QUAD
    sizes = tuple(piece.shape[0] for piece in pieces)
    shards = sum(sizes)
    slots = table_layout(shards)[0]
    groups = tuple(t.shape[0] for t in turned)
    quads = sum(groups)
    starts = tuple(state is None for state in states)
    hbm = pl.BlockSpec(memory_space=pl.ANY)
    operands = [table, *pieces, *turned] + [part for state in states if state is not None for part in state]
    if last:
        out_shape = [jax.ShapeDtypeStruct((rows, count * QUAD * HD), bf) for count in groups]
        out_specs = [pl.BlockSpec(memory_space=pltpu.VMEM)] * len(groups)
    else:
        out_shape = []
        for count in groups:
            out_shape.append(jax.ShapeDtypeStruct((count, HD + ONES, wide), f32))
            out_shape.append(jax.ShapeDtypeStruct((count, 8, wide), f32))
        out_specs = [hbm] * len(out_shape)
    result = pl.pallas_call(
        functools.partial(attend_kernel, sizes, groups, starts, last, rows),
        in_specs=[pl.BlockSpec(memory_space=pltpu.SMEM)] + [hbm] * (len(operands) - 1),
        out_specs=out_specs,
        out_shape=out_shape,
        scratch_shapes=[
            pltpu.VMEM((quads, 2 * HD, wide), bf),
            pltpu.VMEM((slots, rows, 2 * HD), bf),
            pltpu.VMEM((quads, HD + ONES, wide), f32),
            pltpu.VMEM((quads, 8, wide), f32),
            pltpu.VMEM((2 * rows, 2 * rows), f32),
            pltpu.VMEM((2 * rows, 2 * rows), bf),
            pltpu.VMEM((8, 2 * rows), f32),
            pltpu.SemaphoreType.DMA((3 * len(groups),)),
            pltpu.SemaphoreType.DMA((2 * shards,)),
            pltpu.SemaphoreType.DMA((2 * len(groups),)),
        ],
        compiler_params=pltpu.CompilerParams(vmem_limit_bytes=48 * 2**20),
        cost_estimate=pl.CostEstimate(flops=shards * rows * rows * 8 * 4 * HD, bytes_accessed=4 * 2**20, transcendentals=0),
        name="attend",
    )(*operands)
    if last:
        return list(result)
    return [tuple(result[2 * n:2 * n + 2]) for n in range(len(groups))]


def make_table(sources_of, wants_of):
    lines = []
    for me, sources in enumerate(sources_of):
        shards = len(sources)
        slots, at_a, at_b, at_live, at_fast, at_slow, size = table_layout(shards)
        line = np.zeros(size, np.int32)
        line[2:at_live] = -1
        line[at_live:at_fast] = 1
        fast, slow, dummies = [], [], []
        used = 0

        def place(members):
            nonlocal used
            modes = []
            for shard, mode in members:
                line[at_a + shard] = used
                used += 1
                modes.append(mode)
            if len(members) % 2:
                line[at_b + members[-1][0]] = used
                line[at_live + used] = 0
                dummies.append(used)
                used += 1
                modes.append(FULL if members[-1][1] == FULL else EMPTY)
            return [((used - len(modes)) // 2 + n, modes[2 * n], modes[2 * n + 1]) for n in range(len(modes) // 2)]

        shared = []
        placed = set()
        for quads, position, skipped in wants_of[me]:
            new = [(n, FULL if source < position else DIAGONAL) for n, source in enumerate(sources)
                   if source <= position and source not in skipped and n not in placed]
            new.sort(key=lambda member: member[1])
            blocks = place(new)
            placed.update(n for n, _ in new)
            for quad in quads:
                for block, one, two in shared + blocks:
                    code = quad + 4 * block
                    if (one, two) == (FULL, FULL):
                        fast.append(code)
                    else:
                        slow.append(code + 256 * one + 1024 * two)
            shared = shared + [b for b in blocks if b[1] == FULL and b[2] == FULL]
        assert used <= slots and len(dummies) <= DUMMIES
        line[0], line[1] = len(fast), len(slow)
        line[2:2 + len(dummies)] = dummies
        line[at_fast:at_fast + len(fast)] = fast
        line[at_slow:at_slow + len(slow)] = slow
        lines.append(line)
    return np.array(lines)


D = 8192
Z = Y = 4
PLANE = Z * Y
BLOCKS = 2 * PLANE
SHARED = 10


def neighbour(i, x=0, z=0, y=0):
    at_x, at_z, at_y = i // PLANE, (i // Y) % Z, i % Y
    return (at_x + x) % 2 * PLANE + (at_z + z) % Z * Y + (at_y + y) % Y


def mirrored(i):
    return BLOCKS - 1 - i


def moved(value, x=0, z=0, y=0):
    return lax.ppermute(value, "ctx", [(i, neighbour(i, x, z, y)) for i in range(BLOCKS)])


def gathered(first, axis, other):
    line = [first] + [moved(first, **{axis: step}) for step in (1, -1, 2)]
    whole = jnp.stack(line)
    lines = [moved(whole, **{other: step}) for step in (1, -1, 2)]
    return [part[None] for part in line[1:]], lines[:2], lines[2:]


def sources_of(me, plane, axis, other):
    base = plane * PLANE + me % PLANE
    line = [neighbour(base, **{axis: -step}) for step in (0, 1, -1, 2)]
    lines = [[neighbour(b, **{other: -step}) for b in line] for step in (1, -1, 2)]
    return line[1:], lines[0] + lines[1], lines[2]


def wants(me, own, foreign, skipped=()):
    found = []
    if own:
        found.append(((0,) if mirrored(me) < SHARED else (0, 1), me, skipped))
    if foreign and me < SHARED:
        found.append(((2,) if own else (0,), mirrored(me), ()))
    return found


def tables():
    everyone = range(BLOCKS)
    start = [[me, neighbour(me, x=1)] for me in everyone]
    stages = [[sources_of(me, 0, "z", "y")[n] + sources_of(me, 1, "y", "z")[n] for me in everyone] for n in range(3)]
    near = [stages[0][me] + start[me] for me in everyone]
    return (
        make_table(start, [wants(me, True, False) for me in everyone]),
        make_table(near, [wants(me, True, True, tuple(start[me])) for me in everyone]),
        make_table(stages[1], [wants(me, True, True) for me in everyone]),
        make_table(stages[2], [wants(me, False, True) for me in everyone]),
        make_table(stages[2], [wants(me, True, False) for me in everyone]),
    )


def shards(stream_one, stream_two, stream_value, short_stream_taps, medium_filter, residual, norm_gain, queries, keys, values):
    rows, width = stream_one.shape
    middle = queries.shape[1] // 2
    me = lax.axis_index("ctx")
    own = pack_call(keys, values)
    other = moved(own, x=1)
    tail = tail_call(stream_one, stream_two, stream_value, short_stream_taps)
    halo = lax.ppermute(tail, "ctx", [(i, i + 1) for i in range(BLOCKS - 1)])
    given = lax.ppermute(queries[:, middle:], "ctx", [(mirrored(i), i) for i in range(SHARED)])
    first = jnp.where(me < PLANE, own, other)
    second = jnp.where(me < PLANE, other, own)
    a = gathered(first, "z", "y")
    b = gathered(second, "y", "z")
    lists = tables()
    start = [own[None], other[None]]
    turned = turn_call(queries)
    state, = attend_call(lists[0], start, [turned], [None])
    foreign = turn_call(given)
    state, lent = attend_call(lists[1], a[0] + b[0] + start, [turned, foreign], [state, None])
    state, lent = attend_call(lists[2], a[1] + b[1], [turned, foreign], [state, lent])
    helped, = attend_call(lists[3], a[2] + b[2], [foreign], [lent], last=True)
    returned = lax.ppermute(helped, "ctx", [(i, mirrored(i)) for i in range(SHARED)])
    halo, helped = lax.optimization_barrier((halo, helped))
    branch, squares = mixer_call(stream_one, stream_two, stream_value, halo, short_stream_taps, reversed_taps(medium_filter), residual)
    sums = jnp.sum(squares, axis=1)
    state, sums = lax.optimization_barrier((state, sums))
    parts = [lax.ppermute(sums, "tp", [(i, i ^ step) for i in range(4)]) for step in (1, 2, 3)]
    kept, = attend_call(lists[4], a[2] + b[2], [turned], [state], last=True)
    later = jnp.where(me > BLOCKS - 1 - SHARED, returned, kept[:, middle:])
    attended = jnp.concatenate([kept[:, :middle], later], axis=1)
    scaling = lax.rsqrt((sums + parts[0] + parts[1] + parts[2]) / D + 1e-06)
    normed = (branch * scaling[:, None] * norm_gain.astype(f32)[None, :]).astype(bf)
    return normed, attended


def solution(mesh):
    in_specs = (P("ctx", "tp"), P("ctx", "tp"), P("ctx", "tp"), P(None, None, "tp"), P("tp", None),
                P("ctx", "tp"), P("tp"), P("ctx", "tp"), P("ctx", "tp"), P("ctx", "tp"))
    return jax.shard_map(shards, mesh=mesh, in_specs=in_specs, out_specs=(P("ctx", "tp"), P("ctx", "tp")), check_vma=False)
```

```python
import functools
import math

import jax
import jax.numpy as jnp
import numpy as np
from jax import lax
from jax.experimental import pallas as pl
from jax.experimental.pallas import tpu as pltpu
from jax.sharding import PartitionSpec as P

f32=jnp.float32; bf=jnp.bfloat16
SHORT=7; GROUP=16; LANES=128; EDGE=16; TAPS=128; BLK=64
LIGHT = pl.CostEstimate(flops=1000, bytes_accessed=1000, transcendentals=0)

def tail_kernel(one, two, val, taps, out, x_scr):
    keep = TAPS
    last = one.shape[0]
    for lanes in range(one.shape[1] // LANES):
        c = slice(lanes * LANES, (lanes + 1) * LANES)
        t = taps[:, :, c].astype(f32)

        def short(ref, which, slot):
            x_scr[slot] = ref[last - keep - EDGE:, c].astype(f32)
            total = t[which, 0:1] * x_scr[slot, EDGE:EDGE + keep, :]
            for j in range(1, SHORT):
                total += t[which, j:j + 1] * x_scr[slot, EDGE - j:EDGE - j + keep, :]
            return total
        out[0:keep, c] = (short(one, 0, 2 * (lanes % 2)) * short(val, 2, 2 * (lanes % 2) + 1)).astype(bf)
    for n, ref in enumerate((one, two, val)):
        out[keep + EDGE * n:keep + EDGE * (n + 1)] = ref[last - EDGE:, :]


def tail_call(one, two, val, taps):
    rows, width = one.shape
    tile = 4 * LANES
    spec = pl.BlockSpec((rows // 2, tile), lambda i: (1, i))
    out_rows = TAPS + 3 * EDGE
    return pl.pallas_call(tail_kernel, grid=(width // tile,),
        in_specs=[spec] * 3 + [pl.BlockSpec((3, SHORT, tile), lambda i: (0, 0, i))],
        out_specs=pl.BlockSpec((out_rows, tile), lambda i: (0, i)),
        out_shape=jax.ShapeDtypeStruct((out_rows, width), bf),
        scratch_shapes=[pltpu.VMEM((4, TAPS + EDGE, LANES), f32)],
        cost_estimate=LIGHT,
        name="mixed_tail")(one, two, val, taps)


def mixer_kernel(one, two, val, halo, taps, rev, res, branch, squares, x_scr, m_scr, t_scr):
    rows = one.shape[0]
    t = taps[...].astype(f32)
    def short(ref, n):
        lo = TAPS + EDGE * n
        x_scr[n, 0:EDGE] = halo[lo:lo + EDGE, :].astype(f32)
        x_scr[n, EDGE:] = ref[...].astype(f32)
        total = t[n, 0:1] * x_scr[n, EDGE:, :]
        for j in range(1, SHORT):
            total += t[n, j:j + 1] * x_scr[n, EDGE - j:EDGE - j + rows, :]
        return total
    m_scr[0:TAPS] = halo[0:TAPS]
    m_scr[TAPS:] = (short(one, 0) * short(val, 2)).astype(bf)
    gate = short(two, 1)
    groups = LANES // GROUP
    for g in range(groups):
        row = jnp.broadcast_to(rev[g:g + 1, :], (BLK, 2 * TAPS))
        rolled = pltpu.roll(row, 0, 1, stride=1, stride_axis=0)
        t_scr[g * BLK:(g + 1) * BLK] = rolled.astype(bf)
    lane = lax.broadcasted_iota(jnp.int32, (BLK, LANES), 1) // GROUP
    span = BLK + TAPS
    total = jnp.zeros((8, 128), f32)
    for pair in range(rows // (2 * BLK)):
        at = 2 * BLK * pair
        window = jnp.concatenate([m_scr[at:at + span], m_scr[at + BLK:at + BLK + span]], axis=1)
        wide = jnp.dot(t_scr[:, :span], window, preferred_element_type=f32)
        for half in range(2):
            r = slice(at + BLK * half, at + BLK * (half + 1))
            c = slice(LANES * half, LANES * (half + 1))
            medium = wide[0:BLK, c]
            for g in range(1, groups):
                medium = jnp.where(lane == g, wide[g * BLK:(g + 1) * BLK, c], medium)
            summed = res[r].astype(f32) + gate[r] * medium
            branch[r] = summed
            sq = summed * summed
            @pl.when(pl.program_id(0) == 0)
            def _(): squares[r] = sq
            @pl.when(pl.program_id(0) > 0)
            def _(): squares[r] += sq

def mixer_call(one, two, val, halo, taps, rev, res):
    rows, width = one.shape
    spec = pl.BlockSpec((rows, LANES), lambda i: (0, i))
    groups = LANES // GROUP
    return pl.pallas_call(mixer_kernel, grid=(width // LANES,),
        in_specs=[spec] * 3 + [pl.BlockSpec((halo.shape[0], LANES), lambda i: (0, i)),
            pl.BlockSpec((3, SHORT, LANES), lambda i: (0, 0, i)),
            pl.BlockSpec((groups, 2 * TAPS), lambda i: (i, 0)), spec],
        out_specs=[spec, pl.BlockSpec((rows, LANES), lambda i: (0, 0))],
        out_shape=[jax.ShapeDtypeStruct((rows, width), f32), jax.ShapeDtypeStruct((rows, LANES), f32)],
        scratch_shapes=[pltpu.VMEM((3, EDGE + rows, LANES), f32), pltpu.VMEM((TAPS + rows, LANES), bf),
            pltpu.VMEM((groups * BLK, 2 * TAPS), bf)],
        compiler_params=pltpu.CompilerParams(vmem_limit_bytes=32 * 2**20),
        cost_estimate=LIGHT,
        name="mixer")(one, two, val, halo, taps, rev, res)

def reversed_taps(filters):
    flipped = filters.astype(f32)[:, ::-1]
    return jnp.pad(flipped, ((0, 0), (1, TAPS - 1)))


HD = 128
QUAD = 4
ONES = 16
EMPTY, FULL, DIAGONAL = 0, 1, 2
DUMMIES = 3
SCALE = math.log2(math.e) / math.sqrt(HD)


def pack_kernel(keys, values, queries, packed, given, sem):
    middle = given.shape[1]
    copy = pltpu.make_async_copy(queries.at[:, middle:], given, sem)
    copy.start()
    packed[:, :HD] = keys[...]
    turned = values[...].astype(f32).T.astype(bf)
    for part in range(values.shape[0] // HD):
        packed[part * HD:(part + 1) * HD, HD:] = turned[:, part * HD:(part + 1) * HD]
    copy.wait()


def pack_call(keys, values, queries):
    hbm = pl.BlockSpec(memory_space=pltpu.HBM)
    vmem = pl.BlockSpec(memory_space=pltpu.VMEM)
    return pl.pallas_call(pack_kernel, in_specs=[vmem, vmem, hbm], out_specs=[vmem, hbm],
                          out_shape=[jax.ShapeDtypeStruct((keys.shape[0], 2 * HD), bf),
                                     jax.ShapeDtypeStruct((queries.shape[0], queries.shape[1] // 2), bf)],
                          scratch_shapes=[pltpu.SemaphoreType.DMA], name="pack_keys")(keys, values, queries)


def turn_kernel(queries, turned):
    rows = queries.shape[0]
    for head in range(QUAD):
        wide = queries[:, head * HD:(head + 1) * HD].astype(f32).T * SCALE
        high = wide.astype(bf)
        columns = slice(head * rows, (head + 1) * rows)
        turned[0, :HD, columns] = high
        turned[0, HD:, columns] = (wide - high.astype(f32)).astype(bf)


def turn_call(queries):
    rows, width = queries.shape
    quads = width // (QUAD * HD)
    return pl.pallas_call(turn_kernel, grid=(quads,),
        in_specs=[pl.BlockSpec((rows, QUAD * HD), lambda i: (0, i))],
        out_specs=pl.BlockSpec((1, 2 * HD, QUAD * rows), lambda i: (i, 0, 0)),
        out_shape=jax.ShapeDtypeStruct((quads, 2 * HD, QUAD * rows), bf),
        cost_estimate=LIGHT,
        name="turn_queries")(queries)


def table_layout(shards):
    slots = shards + DUMMIES + (shards + DUMMIES) % 2
    at_a = 2 + DUMMIES
    at_b = at_a + shards
    at_live = at_b + shards
    at_fast = at_live + slots
    at_slow = at_fast + 3 * (slots // 2)
    return slots, at_a, at_b, at_live, at_fast, at_slow, at_slow + 3 * (slots // 2)


def attend_kernel(sizes, groups, starts, last, rows, *refs):
    refs = list(refs)
    take = lambda n: [refs.pop(0) for _ in range(n)]
    table, = take(1)
    pieces = take(len(sizes))
    q_in = take(len(groups))
    state_in = [None if start else take(2) for start in starts]
    results = take(len(groups)) if last else [take(2) for _ in groups]
    q, kv, acc, top, s_scr, p_scr, a_scr, load_sem, kv_sem, store_sem = refs
    shards = sum(sizes)
    slots, at_a, at_b, at_live, at_fast, at_slow, _ = table_layout(shards)
    me = lax.axis_index("ctx")
    n_fast = table[me, 0]
    n_slow = table[me, 1]
    half = 2 * rows
    parts = rows // HD

    copies = []
    number = 0
    for piece, size in zip(pieces, sizes):
        for index in range(size):
            for n, at in enumerate((at_a, at_b)):
                slot = table[me, at + number]
                copies.append((slot, pltpu.make_async_copy(
                    piece.at[index], kv.at[jnp.maximum(slot, 0)], kv_sem.at[2 * number + n])))
            number += 1
    for slot, copy in copies:
        pl.when(slot >= 0)(copy.start)
    loads = []
    at = 0
    for n, count in enumerate(groups):
        group = pl.ds(at, count)
        loads.append(pltpu.make_async_copy(q_in[n], q.at[group], load_sem.at[3 * n]))
        if not starts[n]:
            loads.append(pltpu.make_async_copy(state_in[n][0], acc.at[group], load_sem.at[3 * n + 1]))
            loads.append(pltpu.make_async_copy(state_in[n][1], top.at[group], load_sem.at[3 * n + 2]))
        at += count
    for copy in loads:
        copy.start()
    at = 0
    for n, count in enumerate(groups):
        if starts[n]:
            for quad in range(at, at + count):
                acc[quad] = jnp.zeros(acc.shape[1:], f32)
                top[quad] = jnp.full(top.shape[1:], -1e30, f32)
        at += count
    for slot, copy in copies:
        pl.when(slot >= 0)(copy.wait)
    for copy in loads:
        copy.wait()
    for n in range(DUMMIES):
        slot = table[me, 2 + n]

        @pl.when(slot >= 0)
        def _():
            kv[slot, :, HD:] = jnp.zeros((rows, HD), bf)

    def decode(code):
        return code % 4, (code // 4) % 64, (code // 256) % 4, (code // 1024) % 4

    def columns(pair):
        return slice(pair * half, (pair + 1) * half)

    def multiply_keys(quad, block, pair):
        k = jnp.concatenate([kv[2 * block, :, :HD], kv[2 * block + 1, :, :HD]], axis=0)
        k = jnp.concatenate([k, k], axis=1)
        return jnp.dot(k, q[quad, :, columns(pair)], preferred_element_type=f32)

    def multiply_values(quad, block, pair, weights, factor):
        v = jnp.concatenate([kv[2 * block + n // parts, (n % parts) * HD:(n % parts + 1) * HD, HD:]
                             for n in range(2 * parts)], axis=1)
        live = [jnp.full((ONES, rows), table[me, at_live + 2 * block + n].astype(f32)).astype(bf) for n in range(2)]
        v = jnp.concatenate([v, jnp.concatenate(live, axis=1)], axis=0)
        c = columns(pair)
        acc[quad, :, c] = acc[quad, :, c] * factor + jnp.dot(v, weights, preferred_element_type=f32)

    def soften(quad, pair, s):
        c = columns(pair)
        old = top[quad, 0:1, c]
        new = jnp.maximum(old, jnp.max(s, axis=0, keepdims=True))
        top[quad, 0:1, c] = new
        return jnp.exp2(s - new).astype(bf), jnp.exp2(old - new)

    @pl.loop(0, n_slow)
    def _(number):
        quad, block, *modes = decode(table[me, at_slow + number])
        for pair in range(2):
            s_scr[...] = multiply_keys(quad, block, pair)
            key = lax.broadcasted_iota(jnp.int32, (rows, rows), 0)
            query = lax.broadcasted_iota(jnp.int32, (rows, rows), 1)
            for part, mode in enumerate(modes):
                limit = jnp.where(mode == FULL, rows, jnp.where(mode == DIAGONAL, 0, -2 * rows))
                allowed = key - query <= limit
                for head in range(2):
                    r = slice(part * rows, (part + 1) * rows)
                    c = slice(head * rows, (head + 1) * rows)
                    s_scr[r, c] = jnp.where(allowed, s_scr[r, c], -1e30)
            weights, factor = soften(quad, pair, s_scr[...])
            multiply_values(quad, block, pair, weights, factor)

    def fast_entry(number):
        return decode(table[me, at_fast + jnp.clip(number, 0, n_fast - 1)])[:2]

    def region(number, unroll):
        todo = [(*fast_entry(number + n), pair) for n in range(unroll) for pair in range(2)]
        todo.append((*fast_entry(number + unroll), 0))
        s = s_scr[...]
        pending = (*fast_entry(number - 1), 1, p_scr[...], a_scr[0:1])
        for now, later in zip(todo, todo[1:]):
            coming = multiply_keys(*later)
            multiply_values(*pending)
            quad, block, pair = now
            weights, factor = soften(quad, pair, s)
            pending = (quad, block, pair, weights, factor)
            s = coming
        s_scr[...] = s
        p_scr[...] = pending[3]
        a_scr[0:1] = pending[4]

    @pl.when(n_fast > 0)
    def _():
        s_scr[...] = multiply_keys(*fast_entry(0), 0)
        p_scr[...] = jnp.zeros_like(p_scr)
        a_scr[...] = jnp.ones_like(a_scr)

        @pl.loop(0, n_fast // 2)
        def _(step):
            region(2 * step, 2)

        @pl.when(n_fast % 2 == 1)
        def _():
            region(n_fast - 1, 1)

        multiply_values(*fast_entry(n_fast - 1), 1, p_scr[...], a_scr[0:1])

    if last:
        at = 0
        for n, count in enumerate(groups):
            for quad in range(count):
                for head in range(QUAD):
                    c = slice(head * rows, (head + 1) * rows)
                    value = acc[at + quad, :HD, c] / acc[at + quad, HD:HD + 1, c]
                    to = (quad * QUAD + head) * HD
                    results[n][:, to:to + HD] = value.T.astype(bf)
            at += count
    else:
        stores = []
        at = 0
        for n, count in enumerate(groups):
            group = pl.ds(at, count)
            stores.append(pltpu.make_async_copy(acc.at[group], results[n][0], store_sem.at[2 * n]))
            stores.append(pltpu.make_async_copy(top.at[group], results[n][1], store_sem.at[2 * n + 1]))
            at += count
        for copy in stores:
            copy.start()
        for copy in stores:
            copy.wait()


def attend_call(table, pieces, turned, states, last=False):
    wide = turned[0].shape[2]
    rows = wide // QUAD
    sizes = tuple(piece.shape[0] for piece in pieces)
    shards = sum(sizes)
    slots = table_layout(shards)[0]
    groups = tuple(t.shape[0] for t in turned)
    quads = sum(groups)
    starts = tuple(state is None for state in states)
    hbm = pl.BlockSpec(memory_space=pltpu.HBM)
    operands = [table, *pieces, *turned] + [part for state in states if state is not None for part in state]
    if last:
        out_shape = [jax.ShapeDtypeStruct((rows, count * QUAD * HD), bf) for count in groups]
        out_specs = [pl.BlockSpec(memory_space=pltpu.VMEM)] * len(groups)
    else:
        out_shape = []
        for count in groups:
            out_shape.append(jax.ShapeDtypeStruct((count, HD + ONES, wide), f32))
            out_shape.append(jax.ShapeDtypeStruct((count, 8, wide), f32))
        out_specs = [hbm] * len(out_shape)
    result = pl.pallas_call(
        functools.partial(attend_kernel, sizes, groups, starts, last, rows),
        in_specs=[pl.BlockSpec(memory_space=pltpu.SMEM)] + [hbm] * (len(operands) - 1),
        out_specs=out_specs,
        out_shape=out_shape,
        scratch_shapes=[
            pltpu.VMEM((quads, 2 * HD, wide), bf),
            pltpu.VMEM((slots, rows, 2 * HD), bf),
            pltpu.VMEM((quads, HD + ONES, wide), f32),
            pltpu.VMEM((quads, 8, wide), f32),
            pltpu.VMEM((2 * rows, 2 * rows), f32),
            pltpu.VMEM((2 * rows, 2 * rows), bf),
            pltpu.VMEM((8, 2 * rows), f32),
            pltpu.SemaphoreType.DMA((3 * len(groups),)),
            pltpu.SemaphoreType.DMA((2 * shards,)),
            pltpu.SemaphoreType.DMA((2 * len(groups),)),
        ],
        compiler_params=pltpu.CompilerParams(vmem_limit_bytes=48 * 2**20),
        cost_estimate=LIGHT,
        name="attend",
    )(*operands)
    if last:
        return list(result)
    return [tuple(result[2 * n:2 * n + 2]) for n in range(len(groups))]


def make_table(sources_of, wants_of):
    lines = []
    for me, sources in enumerate(sources_of):
        shards = len(sources)
        slots, at_a, at_b, at_live, at_fast, at_slow, size = table_layout(shards)
        line = np.zeros(size, np.int32)
        line[2:at_live] = -1
        line[at_live:at_fast] = 1
        fast, slow, dummies = [], [], []
        used = 0

        def place(members):
            nonlocal used
            modes = []
            for shard, mode in members:
                line[at_a + shard] = used
                used += 1
                modes.append(mode)
            if len(members) % 2:
                line[at_b + members[-1][0]] = used
                line[at_live + used] = 0
                dummies.append(used)
                used += 1
                modes.append(FULL if members[-1][1] == FULL else EMPTY)
            return [((used - len(modes)) // 2 + n, modes[2 * n], modes[2 * n + 1]) for n in range(len(modes) // 2)]

        shared = []
        placed = set()
        for quads, position, skipped in wants_of[me]:
            new = [(n, FULL if source < position else DIAGONAL) for n, source in enumerate(sources)
                   if source <= position and source not in skipped and n not in placed]
            new.sort(key=lambda member: member[1])
            blocks = place(new)
            placed.update(n for n, _ in new)
            for quad in quads:
                for block, one, two in shared + blocks:
                    code = quad + 4 * block
                    if (one, two) == (FULL, FULL):
                        fast.append(code)
                    else:
                        slow.append(code + 256 * one + 1024 * two)
            shared = shared + [(block, FULL, FULL) for block, _, _ in blocks]
        assert used <= slots and len(dummies) <= DUMMIES
        line[0], line[1] = len(fast), len(slow)
        line[2:2 + len(dummies)] = dummies
        line[at_fast:at_fast + len(fast)] = fast
        line[at_slow:at_slow + len(slow)] = slow
        lines.append(line)
    return np.array(lines)


D = 8192
Z = Y = 4
PLANE = Z * Y
BLOCKS = 2 * PLANE
SHARED = 9


def neighbour(i, x=0, z=0, y=0):
    at_x, at_z, at_y = i // PLANE, (i // Y) % Z, i % Y
    return (at_x + x) % 2 * PLANE + (at_z + z) % Z * Y + (at_y + y) % Y


def mirrored(i):
    return BLOCKS - 1 - i


def moved(value, x=0, z=0, y=0):
    return lax.ppermute(value, "ctx", [(i, neighbour(i, x, z, y)) for i in range(BLOCKS)])


def near_line(first, last, axis):
    return [first, moved(first, **{axis: 1}), moved(first, **{axis: -1}), moved(last, **{axis: 2})]


def sources_of(me, plane, axis, other):
    base = neighbour(me, x=plane)
    line = [neighbour(base, **{axis: -step}) for step in (0, 1, -1, 2)]
    lines = [[neighbour(b, **{other: -step}) for b in line] for step in (1, -1, 2)]
    return [base] + line[1:], lines[0] + lines[1], lines[2]


def wants(me):
    found = [((0,) if mirrored(me) < SHARED else (0, 1), me, ())]
    if me < SHARED:
        found.append(((2,), mirrored(me), ()))
    return found


def tables():
    everyone = range(BLOCKS)
    stages = [[sources_of(me, 0, "z", "y")[n] + sources_of(me, 1, "y", "z")[n] for me in everyone] for n in range(3)]
    return [make_table(stage, [wants(me) for me in everyone]) for stage in stages]


def shards(stream_one, stream_two, stream_value, short_stream_taps, medium_filter, residual, norm_gain, queries, keys, values):
    rows, width = stream_one.shape
    middle = queries.shape[1] // 2
    me = lax.axis_index("ctx")
    own, given = pack_call(keys, values, queries)
    other = moved(own, x=1)
    given = lax.ppermute(given, "ctx", [(mirrored(i), i) for i in range(SHARED)])
    same, other = lax.optimization_barrier((own, other))
    a = near_line(same, same, "z")
    b = near_line(other, other, "y")
    a, b = lax.optimization_barrier((a, b))
    a_line, b_line = jnp.stack(a), jnp.stack(b)
    lines = [moved(a_line, y=1), moved(a_line, y=-1), moved(b_line, z=1), moved(b_line, z=-1)]
    tail = tail_call(stream_one, stream_two, stream_value, short_stream_taps)
    halo = lax.ppermute(tail, "ctx", [(i, i + 1) for i in range(BLOCKS - 1)])
    near, far, across = tables()
    turned = [turn_call(queries), turn_call(given)]
    states = attend_call(near, [part[None] for part in a + b], turned, [None, None])
    a_line, b_line, states = lax.optimization_barrier((a_line, b_line, states))
    crossed = [moved(a_line, y=2), moved(b_line, z=2)]
    states = attend_call(far, lines, turned, states)
    kept, helped = attend_call(across, crossed, turned, states, last=True)
    returned = lax.ppermute(helped, "ctx", [(i, mirrored(i)) for i in range(SHARED)])
    halo, helped = lax.optimization_barrier((halo, helped))
    branch, squares = mixer_call(stream_one, stream_two, stream_value, halo, short_stream_taps, reversed_taps(medium_filter), residual)
    sums = jnp.sum(squares, axis=1)
    sums, returned = lax.optimization_barrier((sums, returned))
    parts = [lax.ppermute(sums, "tp", [(i, i ^ step) for i in range(4)]) for step in (1, 2, 3)]
    later = jnp.where(me > BLOCKS - 1 - SHARED, returned, kept[:, middle:])
    attended = jnp.concatenate([kept[:, :middle], later], axis=1)
    scaling = lax.rsqrt((sums + parts[0] + parts[1] + parts[2]) / D + 1e-06)
    normed = (branch * scaling[:, None] * norm_gain.astype(f32)[None, :]).astype(bf)
    return normed, attended


def solution(mesh):
    in_specs = (P("ctx", "tp"), P("ctx", "tp"), P("ctx", "tp"), P(None, None, "tp"), P("tp", None),
                P("ctx", "tp"), P("tp"), P("ctx", "tp"), P("ctx", "tp"), P("ctx", "tp"))
    return jax.shard_map(shards, mesh=mesh, in_specs=in_specs, out_specs=(P("ctx", "tp"), P("ctx", "tp")), check_vma=False)
```

```python
import functools
import math

import jax
import jax.numpy as jnp
import numpy as np
from jax import lax
from jax.experimental import pallas as pl
from jax.experimental.pallas import tpu as pltpu
from jax.sharding import PartitionSpec as P

f32=jnp.float32; bf=jnp.bfloat16
SHORT=7; GROUP=16; LANES=128; EDGE=16; TAPS=128; BLK=64
VMEM = 60 * 2**20
ATTEND_VMEM = 28 * 2**20
LIGHT = pl.CostEstimate(flops=1000, bytes_accessed=1000, transcendentals=0)
PARAMS = pltpu.CompilerParams(vmem_limit_bytes=VMEM)

def tail_kernel(one, two, val, taps, out, streams, x_scr, sems):
    keep = TAPS
    first = one.shape[0] - keep - EDGE
    copies = [pltpu.make_async_copy(ref.at[first:], streams.at[n], sems.at[n]) for n, ref in enumerate((one, val, two))]
    for copy in copies:
        copy.start()
    for copy in copies:
        copy.wait()
    for lanes in range(one.shape[1] // LANES):
        c = slice(lanes * LANES, (lanes + 1) * LANES)
        t = taps[:, :, c].astype(f32)

        def short(stream, which, slot):
            x_scr[slot] = streams[stream, :, c].astype(f32)
            total = t[which, 0:1] * x_scr[slot, EDGE:EDGE + keep, :]
            for j in range(1, SHORT):
                total += t[which, j:j + 1] * x_scr[slot, EDGE - j:EDGE - j + keep, :]
            return total
        slot = 2 * (lanes % 4)
        out[0:keep, c] = (short(0, 0, slot) * short(1, 2, slot + 1)).astype(bf)
    for n, stream in enumerate((0, 2, 1)):
        out[keep + EDGE * n:keep + EDGE * (n + 1)] = streams[stream, keep:]


def tail_call(one, two, val, taps):
    rows, width = one.shape
    hbm = pl.BlockSpec(memory_space=pltpu.HBM)
    vmem = pl.BlockSpec(memory_space=pltpu.VMEM)
    return pl.pallas_call(tail_kernel, in_specs=[hbm] * 3 + [vmem], out_specs=vmem,
        out_shape=jax.ShapeDtypeStruct((TAPS + 3 * EDGE, width), bf),
        scratch_shapes=[pltpu.VMEM((3, TAPS + EDGE, width), bf), pltpu.VMEM((8, TAPS + EDGE, LANES), f32),
                        pltpu.SemaphoreType.DMA((3,))],
        compiler_params=pltpu.CompilerParams(vmem_limit_bytes=ATTEND_VMEM),
        cost_estimate=LIGHT,
        name="mixed_tail")(one, two, val, taps)


def mixer_kernel(one, two, val, halo, taps, rev, res, branch, squares, x_scr, m_scr, t_scr):
    rows = one.shape[0]
    groups = LANES // GROUP
    span = BLK + TAPS
    lane = lax.broadcasted_iota(jnp.int32, (BLK, LANES), 1) // GROUP
    for unit in range(one.shape[1] // LANES):
        lanes = slice(unit * LANES, (unit + 1) * LANES)
        t = taps[:, :, lanes].astype(f32)

        def short(ref, n):
            lo = TAPS + EDGE * n
            x_scr[unit, n, 0:EDGE] = halo[lo:lo + EDGE, lanes].astype(f32)
            x_scr[unit, n, EDGE:] = ref[:, lanes].astype(f32)
            total = t[n, 0:1] * x_scr[unit, n, EDGE:, :]
            for j in range(1, SHORT):
                total += t[n, j:j + 1] * x_scr[unit, n, EDGE - j:EDGE - j + rows, :]
            return total
        m_scr[unit, 0:TAPS] = halo[0:TAPS, lanes]
        m_scr[unit, TAPS:] = (short(one, 0) * short(val, 2)).astype(bf)
        gate = short(two, 1)
        for g in range(groups):
            row = jnp.broadcast_to(rev[unit * groups + g:unit * groups + g + 1, :], (BLK, 2 * TAPS))
            rolled = pltpu.roll(row, 0, 1, stride=1, stride_axis=0)
            t_scr[unit, g * BLK:(g + 1) * BLK] = rolled.astype(bf)
        for pair in range(rows // (2 * BLK)):
            at = 2 * BLK * pair
            window = jnp.concatenate([m_scr[unit, at:at + span], m_scr[unit, at + BLK:at + BLK + span]], axis=1)
            wide = jnp.dot(t_scr[unit, :, :span], window, preferred_element_type=f32)
            for half in range(2):
                r = slice(at + BLK * half, at + BLK * (half + 1))
                c = slice(LANES * half, LANES * (half + 1))
                medium = wide[0:BLK, c]
                for g in range(1, groups):
                    medium = jnp.where(lane == g, wide[g * BLK:(g + 1) * BLK, c], medium)
                summed = res[r, lanes].astype(f32) + gate[r] * medium
                branch[r, lanes] = summed
                square = summed * summed
                if unit == 0:
                    square += jnp.where(pl.program_id(0) == 0, 0.0, squares[r])
                else:
                    square += squares[r]
                squares[r] = square


def mixer_call(one, two, val, halo, taps, rev, res):
    rows, width = one.shape
    units = 4
    tile = units * LANES
    groups = tile // GROUP
    spec = pl.BlockSpec((rows, tile), lambda i: (0, i))
    return pl.pallas_call(mixer_kernel, grid=(width // tile,),
        in_specs=[spec] * 3 + [pl.BlockSpec((halo.shape[0], tile), lambda i: (0, i)),
            pl.BlockSpec((3, SHORT, tile), lambda i: (0, 0, i)),
            pl.BlockSpec((groups, 2 * TAPS), lambda i: (i, 0)), spec],
        out_specs=[spec, pl.BlockSpec((rows, LANES), lambda i: (0, 0))],
        out_shape=[jax.ShapeDtypeStruct((rows, width), f32), jax.ShapeDtypeStruct((rows, LANES), f32)],
        scratch_shapes=[pltpu.VMEM((units, 3, EDGE + rows, LANES), f32), pltpu.VMEM((units, TAPS + rows, LANES), bf),
            pltpu.VMEM((units, LANES // GROUP * BLK, 2 * TAPS), bf)],
        compiler_params=PARAMS,
        cost_estimate=LIGHT,
        name="mixer")(one, two, val, halo, taps, rev, res)


def reversed_taps(filters):
    flipped = filters.astype(f32)[:, ::-1]
    return jnp.pad(flipped, ((0, 0), (1, TAPS - 1)))


HD = 128
QUAD = 4
ONES = 16
EMPTY, FULL, DIAGONAL = 0, 1, 2
DUMMIES = 3
SCALE = math.log2(math.e) / math.sqrt(HD)


def pack_kernel(keys, values, queries, packed, given):
    packed[:, :HD] = keys[...]
    turned = values[...].astype(f32).T.astype(bf)
    for part in range(values.shape[0] // HD):
        packed[part * HD:(part + 1) * HD, HD:] = turned[:, part * HD:(part + 1) * HD]
    given[...] = queries[...]


def pack_call(keys, values, queries):
    rows, width = queries.shape
    shape = (rows, width // 2)
    whole = lambda i: (0, 0)
    return pl.pallas_call(pack_kernel, grid=(1,),
        in_specs=[pl.BlockSpec(keys.shape, whole), pl.BlockSpec(values.shape, whole), pl.BlockSpec(shape, lambda i: (0, 1))],
        out_specs=[pl.BlockSpec((rows, 2 * HD), whole), pl.BlockSpec(shape, whole)],
        out_shape=[jax.ShapeDtypeStruct((rows, 2 * HD), bf), jax.ShapeDtypeStruct(shape, bf)],
        compiler_params=PARAMS, cost_estimate=LIGHT, name="pack_keys")(keys, values, queries)


def turn_kernel(queries, turned):
    rows = queries.shape[0]
    for head in range(QUAD):
        wide = queries[:, head * HD:(head + 1) * HD].astype(f32).T * SCALE
        high = wide.astype(bf)
        columns = slice(head * rows, (head + 1) * rows)
        turned[0, :HD, columns] = high
        turned[0, HD:, columns] = (wide - high.astype(f32)).astype(bf)


def turn_call(queries):
    rows, width = queries.shape
    quads = width // (QUAD * HD)
    return pl.pallas_call(turn_kernel, grid=(quads,),
        in_specs=[pl.BlockSpec((rows, QUAD * HD), lambda i: (0, i))],
        out_specs=pl.BlockSpec((1, 2 * HD, QUAD * rows), lambda i: (i, 0, 0)),
        out_shape=jax.ShapeDtypeStruct((quads, 2 * HD, QUAD * rows), bf),
        compiler_params=pltpu.CompilerParams(vmem_limit_bytes=ATTEND_VMEM), cost_estimate=LIGHT,
        name="turn_queries")(queries)


def table_layout(shards):
    slots = shards + DUMMIES + (shards + DUMMIES) % 2
    at_a = 2 + DUMMIES
    at_b = at_a + shards
    at_live = at_b + shards
    at_fast = at_live + slots
    at_slow = at_fast + 3 * (slots // 2)
    return slots, at_a, at_b, at_live, at_fast, at_slow, at_slow + 3 * (slots // 2)


def attend_kernel(sizes, groups, starts, last, rows, *refs):
    refs = list(refs)
    take = lambda n: [refs.pop(0) for _ in range(n)]
    table, = take(1)
    pieces = take(len(sizes))
    q_in = take(len(groups))
    state_in = [None if start else take(2) for start in starts]
    results = take(len(groups)) if last else [take(2) for _ in groups]
    q, kv, acc, top, s_scr, p_scr, a_scr, load_sem, kv_sem, store_sem = refs
    shards = sum(sizes)
    slots, at_a, at_b, at_live, at_fast, at_slow, _ = table_layout(shards)
    me = lax.axis_index("ctx")
    n_fast = table[me, 0]
    n_slow = table[me, 1]
    half = 2 * rows
    parts = rows // HD

    copies = []
    number = 0
    for piece, size in zip(pieces, sizes):
        for index in range(size):
            for n, at in enumerate((at_a, at_b)):
                slot = table[me, at + number]
                copies.append((slot, pltpu.make_async_copy(
                    piece.at[index], kv.at[jnp.maximum(slot, 0)], kv_sem.at[2 * number + n])))
            number += 1
    for slot, copy in copies:
        pl.when(slot >= 0)(copy.start)
    loads = []
    at = 0
    for n, count in enumerate(groups):
        group = pl.ds(at, count)
        loads.append(pltpu.make_async_copy(q_in[n], q.at[group], load_sem.at[3 * n]))
        if not starts[n]:
            loads.append(pltpu.make_async_copy(state_in[n][0], acc.at[group], load_sem.at[3 * n + 1]))
            loads.append(pltpu.make_async_copy(state_in[n][1], top.at[group], load_sem.at[3 * n + 2]))
        at += count
    for copy in loads:
        copy.start()
    at = 0
    for n, count in enumerate(groups):
        if starts[n]:
            for quad in range(at, at + count):
                acc[quad] = jnp.zeros(acc.shape[1:], f32)
                top[quad] = jnp.full(top.shape[1:], -1e30, f32)
        at += count
    for slot, copy in copies:
        pl.when(slot >= 0)(copy.wait)
    for copy in loads:
        copy.wait()
    for n in range(DUMMIES):
        slot = table[me, 2 + n]

        @pl.when(slot >= 0)
        def _():
            kv[slot, :, HD:] = jnp.zeros((rows, HD), bf)

    def decode(code):
        return code % 4, (code // 4) % 64, (code // 256) % 4, (code // 1024) % 4

    def columns(pair):
        return slice(pair * half, (pair + 1) * half)

    def multiply_keys(quad, block, pair):
        k = jnp.concatenate([kv[2 * block, :, :HD], kv[2 * block + 1, :, :HD]], axis=0)
        k = jnp.concatenate([k, k], axis=1)
        return jnp.dot(k, q[quad, :, columns(pair)], preferred_element_type=f32)

    def multiply_values(quad, block, pair, weights, factor):
        v = jnp.concatenate([kv[2 * block + n // parts, (n % parts) * HD:(n % parts + 1) * HD, HD:]
                             for n in range(2 * parts)], axis=1)
        live = [jnp.full((ONES, rows), table[me, at_live + 2 * block + n].astype(f32)).astype(bf) for n in range(2)]
        v = jnp.concatenate([v, jnp.concatenate(live, axis=1)], axis=0)
        c = columns(pair)
        acc[quad, :, c] = acc[quad, :, c] * factor + jnp.dot(v, weights, preferred_element_type=f32)

    def soften(quad, pair, s):
        c = columns(pair)
        old = top[quad, 0:1, c]
        new = jnp.maximum(old, jnp.max(s, axis=0, keepdims=True))
        top[quad, 0:1, c] = new
        return jnp.exp2(s - new).astype(bf), jnp.exp2(old - new)

    @pl.loop(0, n_slow)
    def _(number):
        quad, block, *modes = decode(table[me, at_slow + number])
        lead = (lax.broadcasted_iota(jnp.int32, (rows, rows), 0) - lax.broadcasted_iota(jnp.int32, (rows, rows), 1))
        lead = jnp.concatenate([lead, lead], axis=1)
        limits = [jnp.where(mode == FULL, rows, jnp.where(mode == DIAGONAL, 0, -2 * rows)) for mode in modes]
        for pair in range(2):
            s = multiply_keys(quad, block, pair)
            s = jnp.concatenate([jnp.where(lead <= limits[n], s[n * rows:(n + 1) * rows], -1e30) for n in range(2)], axis=0)
            weights, factor = soften(quad, pair, s)
            multiply_values(quad, block, pair, weights, factor)

    def fast_entry(number):
        return decode(table[me, at_fast + jnp.clip(number, 0, n_fast - 1)])[:2]

    def region(number, unroll):
        todo = [(*fast_entry(number + n), pair) for n in range(unroll) for pair in range(2)]
        todo.append((*fast_entry(number + unroll), 0))
        s = s_scr[...]
        pending = (*fast_entry(number - 1), 1, p_scr[...], a_scr[0:1])
        for now, later in zip(todo, todo[1:]):
            coming = multiply_keys(*later)
            multiply_values(*pending)
            quad, block, pair = now
            weights, factor = soften(quad, pair, s)
            pending = (quad, block, pair, weights, factor)
            s = coming
        s_scr[...] = s
        p_scr[...] = pending[3]
        a_scr[0:1] = pending[4]

    @pl.when(n_fast > 0)
    def _():
        s_scr[...] = multiply_keys(*fast_entry(0), 0)
        p_scr[...] = jnp.zeros_like(p_scr)
        a_scr[...] = jnp.ones_like(a_scr)

        @pl.loop(0, n_fast // 2)
        def _(step):
            region(2 * step, 2)

        @pl.when(n_fast % 2 == 1)
        def _():
            region(n_fast - 1, 1)

        multiply_values(*fast_entry(n_fast - 1), 1, p_scr[...], a_scr[0:1])

    if last:
        at = 0
        for n, count in enumerate(groups):
            for quad in range(count):
                for head in range(QUAD):
                    c = slice(head * rows, (head + 1) * rows)
                    value = acc[at + quad, :HD, c] * (1.0 / acc[at + quad, HD:HD + 1, c])
                    to = (quad * QUAD + head) * HD
                    results[n][:, to:to + HD] = value.T.astype(bf)
            at += count
    else:
        stores = []
        at = 0
        for n, count in enumerate(groups):
            group = pl.ds(at, count)
            stores.append(pltpu.make_async_copy(acc.at[group], results[n][0], store_sem.at[2 * n]))
            stores.append(pltpu.make_async_copy(top.at[group], results[n][1], store_sem.at[2 * n + 1]))
            at += count
        for copy in stores:
            copy.start()
        for copy in stores:
            copy.wait()


def attend_call(table, pieces, turned, states, last=False):
    wide = turned[0].shape[2]
    rows = wide // QUAD
    sizes = tuple(piece.shape[0] for piece in pieces)
    shards = sum(sizes)
    slots = table_layout(shards)[0]
    groups = tuple(t.shape[0] for t in turned)
    quads = sum(groups)
    starts = tuple(state is None for state in states)
    hbm = pl.BlockSpec(memory_space=pltpu.HBM)
    anywhere = pl.BlockSpec(memory_space=pl.ANY)
    operands = [table, *pieces, *turned] + [part for state in states if state is not None for part in state]
    if last:
        out_shape = [jax.ShapeDtypeStruct((rows, count * QUAD * HD), bf) for count in groups]
        out_specs = [pl.BlockSpec(memory_space=pltpu.VMEM)] * len(groups)
    else:
        out_shape = []
        for count in groups:
            out_shape.append(jax.ShapeDtypeStruct((count, HD + ONES, wide), f32))
            out_shape.append(jax.ShapeDtypeStruct((count, 8, wide), f32))
        out_specs = [hbm] * len(out_shape)
    result = pl.pallas_call(
        functools.partial(attend_kernel, sizes, groups, starts, last, rows),
        in_specs=[pl.BlockSpec(memory_space=pltpu.SMEM)] + [anywhere] * len(pieces) + [hbm] * (len(operands) - 1 - len(pieces)),
        out_specs=out_specs,
        out_shape=out_shape,
        scratch_shapes=[
            pltpu.VMEM((quads, 2 * HD, wide), bf),
            pltpu.VMEM((slots, rows, 2 * HD), bf),
            pltpu.VMEM((quads, HD + ONES, wide), f32),
            pltpu.VMEM((quads, 8, wide), f32),
            pltpu.VMEM((2 * rows, 2 * rows), f32),
            pltpu.VMEM((2 * rows, 2 * rows), bf),
            pltpu.VMEM((8, 2 * rows), f32),
            pltpu.SemaphoreType.DMA((3 * len(groups),)),
            pltpu.SemaphoreType.DMA((2 * shards,)),
            pltpu.SemaphoreType.DMA((2 * len(groups),)),
        ],
        compiler_params=pltpu.CompilerParams(vmem_limit_bytes=ATTEND_VMEM),
        cost_estimate=LIGHT,
        name="attend",
    )(*operands)
    if last:
        return list(result)
    return [tuple(result[2 * n:2 * n + 2]) for n in range(len(groups))]


def make_table(sources_of, wants_of):
    lines = []
    for me, sources in enumerate(sources_of):
        shards = len(sources)
        slots, at_a, at_b, at_live, at_fast, at_slow, size = table_layout(shards)
        line = np.zeros(size, np.int32)
        line[2:at_live] = -1
        line[at_live:at_fast] = 1
        fast, slow, dummies = [], [], []
        used = 0

        def place(members):
            nonlocal used
            modes = []
            for shard, mode in members:
                line[at_a + shard] = used
                used += 1
                modes.append(mode)
            if len(members) % 2:
                line[at_b + members[-1][0]] = used
                line[at_live + used] = 0
                dummies.append(used)
                used += 1
                modes.append(FULL if members[-1][1] == FULL else EMPTY)
            return [((used - len(modes)) // 2 + n, modes[2 * n], modes[2 * n + 1]) for n in range(len(modes) // 2)]

        shared = []
        placed = set()
        for quads, position, skipped in wants_of[me]:
            new = [(n, FULL if source < position else DIAGONAL) for n, source in enumerate(sources)
                   if source <= position and source not in skipped and n not in placed]
            new.sort(key=lambda member: member[1])
            blocks = place(new)
            placed.update(n for n, _ in new)
            for quad in quads:
                for block, one, two in shared + blocks:
                    code = quad + 4 * block
                    if (one, two) == (FULL, FULL):
                        fast.append(code)
                    else:
                        slow.append(code + 256 * one + 1024 * two)
            shared = shared + [(block, FULL, FULL) for block, _, _ in blocks]
        assert used <= slots and len(dummies) <= DUMMIES
        line[0], line[1] = len(fast), len(slow)
        line[2:2 + len(dummies)] = dummies
        line[at_fast:at_fast + len(fast)] = fast
        line[at_slow:at_slow + len(slow)] = slow
        lines.append(line)
    return np.array(lines)


D = 8192
Z = Y = 4
PLANE = Z * Y
BLOCKS = 2 * PLANE
SHARED = 9


def neighbour(i, x=0, z=0, y=0):
    at_x, at_z, at_y = i // PLANE, (i // Y) % Z, i % Y
    return (at_x + x) % 2 * PLANE + (at_z + z) % Z * Y + (at_y + y) % Y


def mirrored(i):
    return BLOCKS - 1 - i


def moved(value, x=0, z=0, y=0):
    return lax.ppermute(value, "ctx", [(i, neighbour(i, x, z, y)) for i in range(BLOCKS)])


def near_line(first, last, axis):
    return [first, moved(first, **{axis: 1}), moved(first, **{axis: -1}), moved(last, **{axis: 2})]


def sources_of(me, plane, axis, other):
    base = neighbour(me, x=plane)
    line = [neighbour(base, **{axis: -step}) for step in (0, 1, -1, 2)]
    lines = [[neighbour(b, **{other: -step}) for b in line] for step in (1, -1, 2)]
    return [base] + line[1:], lines[0] + lines[1], lines[2]


def wants(me):
    found = [((0,) if mirrored(me) < SHARED else (0, 1), me, ())]
    if me < SHARED:
        found.append(((2,), mirrored(me), ()))
    return found


def tables():
    everyone = range(BLOCKS)
    stages = [[sources_of(me, 0, "z", "y")[n] + sources_of(me, 1, "y", "z")[n] for me in everyone] for n in range(3)]
    return [make_table(stage, [wants(me) for me in everyone]) for stage in stages]


def shards(stream_one, stream_two, stream_value, short_stream_taps, medium_filter, residual, norm_gain, queries, keys, values):
    rows, width = stream_one.shape
    middle = queries.shape[1] // 2
    me = lax.axis_index("ctx")
    own, given = pack_call(keys, values, queries)
    other = moved(own, x=1)
    given = lax.ppermute(given, "ctx", [(mirrored(i), i) for i in range(SHARED)])
    same, other = lax.optimization_barrier((own, other))
    a = near_line(same, same, "z")
    b = near_line(other, other, "y")
    a, b = lax.optimization_barrier((a, b))
    a_line, b_line = jnp.stack(a), jnp.stack(b)
    lines = [moved(a_line, y=1), moved(a_line, y=-1), moved(b_line, z=1), moved(b_line, z=-1)]
    tail = tail_call(stream_one, stream_two, stream_value, short_stream_taps)
    halo = lax.ppermute(tail, "ctx", [(i, i + 1) for i in range(BLOCKS - 1)])
    near, far, across = tables()
    turned = [turn_call(queries), turn_call(given)]
    states = attend_call(near, [part[None] for part in a + b], turned, [None, None])
    a_line, b_line, states = lax.optimization_barrier((a_line, b_line, states))
    crossed = [moved(a_line, y=2), moved(b_line, z=2)]
    states = attend_call(far, lines, turned, states)
    kept, helped = attend_call(across, crossed, turned, states, last=True)
    returned = lax.ppermute(helped, "ctx", [(i, mirrored(i)) for i in range(SHARED)])
    halo, helped = lax.optimization_barrier((halo, helped))
    branch, squares = mixer_call(stream_one, stream_two, stream_value, halo, short_stream_taps, reversed_taps(medium_filter), residual)
    sums = jnp.sum(squares, axis=1)
    sums, returned = lax.optimization_barrier((sums, returned))
    parts = [lax.ppermute(sums, "tp", [(i, i ^ step) for i in range(4)]) for step in (1, 2, 3)]
    later = jnp.where(me > BLOCKS - 1 - SHARED, returned, kept[:, middle:])
    attended = jnp.concatenate([kept[:, :middle], later], axis=1)
    scaling = lax.rsqrt((sums + parts[0] + parts[1] + parts[2]) / D + 1e-06)
    normed = (branch * scaling[:, None] * norm_gain.astype(f32)[None, :]).astype(bf)
    return normed, attended


def solution(mesh):
    in_specs = (P("ctx", "tp"), P("ctx", "tp"), P("ctx", "tp"), P(None, None, "tp"), P("tp", None),
                P("ctx", "tp"), P("tp"), P("ctx", "tp"), P("ctx", "tp"), P("ctx", "tp"))
    return jax.shard_map(shards, mesh=mesh, in_specs=in_specs, out_specs=(P("ctx", "tp"), P("ctx", "tp")), check_vma=False)
```

```python
import functools
import math

import jax
import jax.numpy as jnp
import numpy as np
from jax import lax
from jax.experimental import pallas as pl
from jax.experimental.pallas import tpu as pltpu
from jax.sharding import PartitionSpec as P

f32=jnp.float32; bf=jnp.bfloat16
SHORT=7; GROUP=16; LANES=128; EDGE=16; TAPS=128; BLK=64
VMEM = 60 * 2**20
ATTEND_VMEM = 28 * 2**20
LIGHT = pl.CostEstimate(flops=1000, bytes_accessed=1000, transcendentals=0)
PARAMS = pltpu.CompilerParams(vmem_limit_bytes=VMEM)

def tail_kernel(one, two, val, taps, out, streams, x_scr, sems):
    keep = TAPS
    first = one.shape[0] - keep - EDGE
    copies = [pltpu.make_async_copy(ref.at[first:], streams.at[n], sems.at[n]) for n, ref in enumerate((one, val, two))]
    for copy in copies:
        copy.start()
    for copy in copies:
        copy.wait()
    for lanes in range(one.shape[1] // LANES):
        c = slice(lanes * LANES, (lanes + 1) * LANES)
        t = taps[:, :, c].astype(f32)

        def short(stream, which, slot):
            x_scr[slot] = streams[stream, :, c].astype(f32)
            total = t[which, 0:1] * x_scr[slot, EDGE:EDGE + keep, :]
            for j in range(1, SHORT):
                total += t[which, j:j + 1] * x_scr[slot, EDGE - j:EDGE - j + keep, :]
            return total
        slot = 2 * (lanes % 4)
        out[0:keep, c] = (short(0, 0, slot) * short(1, 2, slot + 1)).astype(bf)
    for n, stream in enumerate((0, 2, 1)):
        out[keep + EDGE * n:keep + EDGE * (n + 1)] = streams[stream, keep:]


def tail_call(one, two, val, taps):
    rows, width = one.shape
    hbm = pl.BlockSpec(memory_space=pltpu.HBM)
    vmem = pl.BlockSpec(memory_space=pltpu.VMEM)
    return pl.pallas_call(tail_kernel, in_specs=[hbm] * 3 + [vmem], out_specs=vmem,
        out_shape=jax.ShapeDtypeStruct((TAPS + 3 * EDGE, width), bf),
        scratch_shapes=[pltpu.VMEM((3, TAPS + EDGE, width), bf), pltpu.VMEM((8, TAPS + EDGE, LANES), f32),
                        pltpu.SemaphoreType.DMA((3,))],
        compiler_params=pltpu.CompilerParams(vmem_limit_bytes=ATTEND_VMEM),
        cost_estimate=LIGHT,
        name="mixed_tail")(one, two, val, taps)


def mixer_kernel(one, two, val, halo, taps, rev, res, branch, sums, squares, x_scr, m_scr, t_scr):
    rows = one.shape[0]
    groups = LANES // GROUP
    span = BLK + TAPS
    lane = lax.broadcasted_iota(jnp.int32, (BLK, LANES), 1) // GROUP
    for unit in range(one.shape[1] // LANES):
        lanes = slice(unit * LANES, (unit + 1) * LANES)
        t = taps[:, :, lanes].astype(f32)

        def short(ref, n):
            lo = TAPS + EDGE * n
            x_scr[unit, n, 0:EDGE] = halo[lo:lo + EDGE, lanes].astype(f32)
            x_scr[unit, n, EDGE:] = ref[:, lanes].astype(f32)
            total = t[n, 0:1] * x_scr[unit, n, EDGE:, :]
            for j in range(1, SHORT):
                total += t[n, j:j + 1] * x_scr[unit, n, EDGE - j:EDGE - j + rows, :]
            return total
        m_scr[unit, 0:TAPS] = halo[0:TAPS, lanes]
        m_scr[unit, TAPS:] = (short(one, 0) * short(val, 2)).astype(bf)
        gate = short(two, 1)
        for g in range(groups):
            row = jnp.broadcast_to(rev[unit * groups + g:unit * groups + g + 1, :], (BLK, 2 * TAPS))
            rolled = pltpu.roll(row, 0, 1, stride=1, stride_axis=0)
            t_scr[unit, g * BLK:(g + 1) * BLK] = rolled.astype(bf)
        for pair in range(rows // (2 * BLK)):
            at = 2 * BLK * pair
            window = jnp.concatenate([m_scr[unit, at:at + span], m_scr[unit, at + BLK:at + BLK + span]], axis=1)
            wide = jnp.dot(t_scr[unit, :, :span], window, preferred_element_type=f32)
            for half in range(2):
                r = slice(at + BLK * half, at + BLK * (half + 1))
                c = slice(LANES * half, LANES * (half + 1))
                medium = wide[0:BLK, c]
                for g in range(1, groups):
                    medium = jnp.where(lane == g, wide[g * BLK:(g + 1) * BLK, c], medium)
                summed = res[r, lanes].astype(f32) + gate[r] * medium
                branch[r, lanes] = summed
                square = summed * summed
                if unit == 0:
                    square += jnp.where(pl.program_id(0) == 0, 0.0, squares[r])
                else:
                    square += squares[r]
                squares[r] = square

    @pl.when(pl.program_id(0) == pl.num_programs(0) - 1)
    def _():
        sums[...] = jnp.sum(squares[...].T, axis=0, keepdims=True)


def mixer_call(one, two, val, halo, taps, rev, res):
    rows, width = one.shape
    units = 4
    tile = units * LANES
    groups = tile // GROUP
    spec = pl.BlockSpec((rows, tile), lambda i: (0, i))
    return pl.pallas_call(mixer_kernel, grid=(width // tile,),
        in_specs=[spec] * 3 + [pl.BlockSpec((halo.shape[0], tile), lambda i: (0, i)),
            pl.BlockSpec((3, SHORT, tile), lambda i: (0, 0, i)),
            pl.BlockSpec((groups, 2 * TAPS), lambda i: (i, 0)), spec],
        out_specs=[spec, pl.BlockSpec((1, rows), lambda i: (0, 0))],
        out_shape=[jax.ShapeDtypeStruct((rows, width), f32), jax.ShapeDtypeStruct((1, rows), f32)],
        scratch_shapes=[pltpu.VMEM((rows, LANES), f32), pltpu.VMEM((units, 3, EDGE + rows, LANES), f32), pltpu.VMEM((units, TAPS + rows, LANES), bf),
            pltpu.VMEM((units, LANES // GROUP * BLK, 2 * TAPS), bf)],
        compiler_params=PARAMS,
        cost_estimate=LIGHT,
        name="mixer")(one, two, val, halo, taps, rev, res)


def reversed_taps(filters):
    flipped = filters.astype(f32)[:, ::-1]
    return jnp.pad(flipped, ((0, 0), (1, TAPS - 1)))


HD = 128
UNIT = 2
OWN, LENT = 4, 2
UNITS = OWN + LENT
UNROLL = 4
ONES = 16
EMPTY, FULL, DIAGONAL = 0, 1, 2
DUMMIES = 3
SCALE = math.log2(math.e) / math.sqrt(HD)


def pack_kernel(keys, values, queries, packed, given):
    packed[:, :HD] = keys[...]
    turned = values[...].astype(f32).T.astype(bf)
    for part in range(values.shape[0] // HD):
        packed[part * HD:(part + 1) * HD, HD:] = turned[:, part * HD:(part + 1) * HD]
    given[...] = queries[...]


def pack_call(keys, values, queries):
    rows, width = queries.shape
    shape = (rows, width // 2)
    whole = lambda i: (0, 0)
    return pl.pallas_call(pack_kernel, grid=(1,),
        in_specs=[pl.BlockSpec(keys.shape, whole), pl.BlockSpec(values.shape, whole), pl.BlockSpec(shape, lambda i: (0, 1))],
        out_specs=[pl.BlockSpec((rows, 2 * HD), whole), pl.BlockSpec(shape, whole)],
        out_shape=[jax.ShapeDtypeStruct((rows, 2 * HD), bf), jax.ShapeDtypeStruct(shape, bf)],
        compiler_params=PARAMS, cost_estimate=LIGHT, name="pack_keys")(keys, values, queries)


def turn_kernel(queries, turned):
    rows = queries.shape[0]
    for head in range(UNIT):
        wide = queries[:, head * HD:(head + 1) * HD].astype(f32).T * SCALE
        high = wide.astype(bf)
        columns = slice(head * rows, (head + 1) * rows)
        turned[0, :HD, columns] = high
        turned[0, HD:, columns] = (wide - high.astype(f32)).astype(bf)


def turn_call(queries):
    rows, width = queries.shape
    units = width // (UNIT * HD)
    return pl.pallas_call(turn_kernel, grid=(units,),
        in_specs=[pl.BlockSpec((rows, UNIT * HD), lambda i: (0, i))],
        out_specs=pl.BlockSpec((1, 2 * HD, UNIT * rows), lambda i: (i, 0, 0)),
        out_shape=jax.ShapeDtypeStruct((units, 2 * HD, UNIT * rows), bf),
        compiler_params=pltpu.CompilerParams(vmem_limit_bytes=ATTEND_VMEM), cost_estimate=LIGHT,
        name="turn_queries")(queries)


def table_layout(shards):
    slots = shards + DUMMIES + (shards + DUMMIES) % 2
    at_a = 2 + DUMMIES
    at_b = at_a + shards
    at_live = at_b + shards
    at_fast = at_live + slots
    at_slow = at_fast + UNITS * (slots // 2)
    return slots, at_a, at_b, at_live, at_fast, at_slow, at_slow + UNITS * (slots // 2)


def attend_kernel(sizes, groups, starts, last, rows, *refs):
    refs = list(refs)
    take = lambda n: [refs.pop(0) for _ in range(n)]
    table, = take(1)
    pieces = take(len(sizes))
    q_in = take(len(groups))
    state_in = [None if start else take(2) for start in starts]
    results = take(len(groups)) if last else [take(2) for _ in groups]
    q, kv, acc, top, s_scr, p_scr, a_scr, load_sem, kv_sem, store_sem = refs
    shards = sum(sizes)
    slots, at_a, at_b, at_live, at_fast, at_slow, _ = table_layout(shards)
    me = lax.axis_index("ctx")
    n_fast = table[me, 0]
    n_slow = table[me, 1]
    half = 2 * rows
    parts = rows // HD

    copies = []
    number = 0
    for piece, size in zip(pieces, sizes):
        for index in range(size):
            for n, at in enumerate((at_a, at_b)):
                slot = table[me, at + number]
                copies.append((slot, pltpu.make_async_copy(
                    piece.at[index], kv.at[jnp.maximum(slot, 0)], kv_sem.at[2 * number + n])))
            number += 1
    for slot, copy in copies:
        pl.when(slot >= 0)(copy.start)
    loads = []
    at = 0
    for n, count in enumerate(groups):
        group = pl.ds(at, count)
        loads.append(pltpu.make_async_copy(q_in[n], q.at[group], load_sem.at[3 * n]))
        if not starts[n]:
            loads.append(pltpu.make_async_copy(state_in[n][0], acc.at[group], load_sem.at[3 * n + 1]))
            loads.append(pltpu.make_async_copy(state_in[n][1], top.at[group], load_sem.at[3 * n + 2]))
        at += count
    for copy in loads:
        copy.start()
    at = 0
    for n, count in enumerate(groups):
        if starts[n]:
            for unit in range(at, at + count):
                acc[unit] = jnp.zeros(acc.shape[1:], f32)
                top[unit] = jnp.full(top.shape[1:], -1e30, f32)
        at += count
    for slot, copy in copies:
        pl.when(slot >= 0)(copy.wait)
    for copy in loads:
        copy.wait()
    for n in range(DUMMIES):
        slot = table[me, 2 + n]

        @pl.when(slot >= 0)
        def _():
            kv[slot, :, HD:] = jnp.zeros((rows, HD), bf)

    def decode(code):
        return code % 8, (code // 8) % 64, (code // 512) % 4, (code // 2048) % 4

    def multiply_keys(unit, block):
        k = jnp.concatenate([kv[2 * block, :, :HD], kv[2 * block + 1, :, :HD]], axis=0)
        k = jnp.concatenate([k, k], axis=1)
        return jnp.dot(k, q[unit], preferred_element_type=f32)

    def multiply_values(unit, block, weights, factor):
        v = jnp.concatenate([kv[2 * block + n // parts, (n % parts) * HD:(n % parts + 1) * HD, HD:]
                             for n in range(2 * parts)], axis=1)
        live = [jnp.full((ONES, rows), table[me, at_live + 2 * block + n].astype(f32)).astype(bf) for n in range(2)]
        v = jnp.concatenate([v, jnp.concatenate(live, axis=1)], axis=0)
        acc[unit] = acc[unit] * factor + jnp.dot(v, weights, preferred_element_type=f32)

    def soften(unit, s):
        old = top[unit, 0:1]
        new = jnp.maximum(old, jnp.max(s, axis=0, keepdims=True))
        top[unit, 0:1] = new
        return jnp.exp2(s - new).astype(bf), jnp.exp2(old - new)

    @pl.loop(0, n_slow)
    def _(number):
        unit, block, *modes = decode(table[me, at_slow + number])
        lead = (lax.broadcasted_iota(jnp.int32, (rows, rows), 0) - lax.broadcasted_iota(jnp.int32, (rows, rows), 1))
        lead = jnp.concatenate([lead, lead], axis=1)
        limits = [jnp.where(mode == FULL, rows, jnp.where(mode == DIAGONAL, 0, -2 * rows)) for mode in modes]
        s = multiply_keys(unit, block)
        s = jnp.concatenate([jnp.where(lead <= limits[n], s[n * rows:(n + 1) * rows], -1e30) for n in range(2)], axis=0)
        weights, factor = soften(unit, s)
        multiply_values(unit, block, weights, factor)

    def fast_entry(number):
        return decode(table[me, at_fast + jnp.clip(number, 0, n_fast - 1)])[:2]

    def region(number, unroll):
        todo = [fast_entry(number + n) for n in range(unroll + 1)]
        s = s_scr[...]
        pending = (*fast_entry(number - 1), p_scr[...], a_scr[0:1])
        for (unit, block), later in zip(todo, todo[1:]):
            coming = multiply_keys(*later)
            multiply_values(*pending)
            weights, factor = soften(unit, s)
            pending = (unit, block, weights, factor)
            s = coming
        s_scr[...] = s
        p_scr[...] = pending[2]
        a_scr[0:1] = pending[3]

    @pl.when(n_fast > 0)
    def _():
        s_scr[...] = multiply_keys(*fast_entry(0))
        p_scr[...] = jnp.zeros_like(p_scr)
        a_scr[...] = jnp.ones_like(a_scr)

        @pl.loop(0, n_fast // UNROLL)
        def _(step):
            region(UNROLL * step, UNROLL)

        @pl.when((n_fast // 2) % 2 == 1)
        def _():
            region(n_fast // UNROLL * UNROLL, 2)

        @pl.when(n_fast % 2 == 1)
        def _():
            region(n_fast - 1, 1)

        multiply_values(*fast_entry(n_fast - 1), p_scr[...], a_scr[0:1])

    if last:
        at = 0
        for n, count in enumerate(groups):
            for unit in range(count):
                for head in range(UNIT):
                    c = slice(head * rows, (head + 1) * rows)
                    value = acc[at + unit, :HD, c] * (1.0 / acc[at + unit, HD:HD + 1, c])
                    to = (unit * UNIT + head) * HD
                    results[n][:, to:to + HD] = value.T.astype(bf)
            at += count
    else:
        stores = []
        at = 0
        for n, count in enumerate(groups):
            group = pl.ds(at, count)
            stores.append(pltpu.make_async_copy(acc.at[group], results[n][0], store_sem.at[2 * n]))
            stores.append(pltpu.make_async_copy(top.at[group], results[n][1], store_sem.at[2 * n + 1]))
            at += count
        for copy in stores:
            copy.start()
        for copy in stores:
            copy.wait()


def attend_call(table, pieces, turned, states, last=False):
    wide = turned[0].shape[2]
    rows = wide // UNIT
    sizes = tuple(piece.shape[0] for piece in pieces)
    shards = sum(sizes)
    slots = table_layout(shards)[0]
    groups = tuple(t.shape[0] for t in turned)
    units = sum(groups)
    starts = tuple(state is None for state in states)
    hbm = pl.BlockSpec(memory_space=pltpu.HBM)
    anywhere = pl.BlockSpec(memory_space=pl.ANY)
    operands = [table, *pieces, *turned] + [part for state in states if state is not None for part in state]
    if last:
        out_shape = [jax.ShapeDtypeStruct((rows, count * UNIT * HD), bf) for count in groups]
        out_specs = [pl.BlockSpec(memory_space=pltpu.VMEM)] * len(groups)
    else:
        out_shape = []
        for count in groups:
            out_shape.append(jax.ShapeDtypeStruct((count, HD + ONES, wide), f32))
            out_shape.append(jax.ShapeDtypeStruct((count, 8, wide), f32))
        out_specs = [hbm] * len(out_shape)
    result = pl.pallas_call(
        functools.partial(attend_kernel, sizes, groups, starts, last, rows),
        in_specs=[pl.BlockSpec(memory_space=pltpu.SMEM)] + [anywhere] * len(pieces) + [hbm] * (len(operands) - 1 - len(pieces)),
        out_specs=out_specs,
        out_shape=out_shape,
        scratch_shapes=[
            pltpu.VMEM((units, 2 * HD, wide), bf),
            pltpu.VMEM((slots, rows, 2 * HD), bf),
            pltpu.VMEM((units, HD + ONES, wide), f32),
            pltpu.VMEM((units, 8, wide), f32),
            pltpu.VMEM((2 * rows, 2 * rows), f32),
            pltpu.VMEM((2 * rows, 2 * rows), bf),
            pltpu.VMEM((8, 2 * rows), f32),
            pltpu.SemaphoreType.DMA((3 * len(groups),)),
            pltpu.SemaphoreType.DMA((2 * shards,)),
            pltpu.SemaphoreType.DMA((2 * len(groups),)),
        ],
        compiler_params=pltpu.CompilerParams(vmem_limit_bytes=ATTEND_VMEM),
        cost_estimate=LIGHT,
        name="attend",
    )(*operands)
    if last:
        return list(result)
    return [tuple(result[2 * n:2 * n + 2]) for n in range(len(groups))]


def make_table(sources_of, wants_of):
    lines = []
    for sources, wanted in zip(sources_of, wants_of):
        shards = len(sources)
        slots, at_a, at_b, at_live, at_fast, at_slow, size = table_layout(shards)
        line = np.zeros(size, np.int32)
        line[2:at_live] = -1
        line[at_live:at_fast] = 1
        fast, slow, dummies = [], [], []
        used = 0

        def place(members):
            nonlocal used
            modes = []
            for shard, mode in members:
                line[at_a + shard] = used
                used += 1
                modes.append(mode)
            if len(members) % 2:
                line[at_b + members[-1][0]] = used
                line[at_live + used] = 0
                dummies.append(used)
                used += 1
                modes.append(FULL if members[-1][1] == FULL else EMPTY)
            return [((used - len(modes)) // 2 + n, modes[2 * n], modes[2 * n + 1]) for n in range(len(modes) // 2)]

        shared = []
        placed = set()
        for units, position, skipped in wanted:
            new = [(n, FULL if source < position else DIAGONAL) for n, source in enumerate(sources)
                   if source <= position and source not in skipped and n not in placed]
            new.sort(key=lambda member: member[1])
            blocks = place(new)
            placed.update(n for n, _ in new)
            for unit in units:
                for block, one, two in shared + blocks:
                    code = unit + 8 * block
                    if (one, two) == (FULL, FULL):
                        fast.append(code)
                    else:
                        slow.append(code + 512 * one + 2048 * two)
            shared = shared + [(block, FULL, FULL) for block, _, _ in blocks]
        assert used <= slots and len(dummies) <= DUMMIES
        line[0], line[1] = len(fast), len(slow)
        line[2:2 + len(dummies)] = dummies
        line[at_fast:at_fast + len(fast)] = fast
        line[at_slow:at_slow + len(slow)] = slow
        lines.append(line)
    return np.array(lines)


D = 8192
Z = Y = 4
PLANE = Z * Y
BLOCKS = 2 * PLANE


def neighbour(i, x=0, z=0, y=0):
    at_x, at_z, at_y = i // PLANE, (i // Y) % Z, i % Y
    return (at_x + x) % 2 * PLANE + (at_z + z) % Z * Y + (at_y + y) % Y


def mirrored(i):
    return BLOCKS - 1 - i


def moved(value, x=0, z=0, y=0):
    return lax.ppermute(value, "ctx", [(i, neighbour(i, x, z, y)) for i in range(BLOCKS)])


def near_line(first, last, axis):
    return [first, moved(first, **{axis: 1}), moved(first, **{axis: -1}), moved(last, **{axis: 2})]


def sources_of(me, plane, axis, other):
    base = neighbour(me, x=plane)
    line = [neighbour(base, **{axis: -step}) for step in (0, 1, -1, 2)]
    lines = [[neighbour(b, **{other: -step}) for b in line] for step in (1, -1, 2)]
    return [base] + line[1:], lines[0] + lines[1], lines[2]


def wants(me, lent):
    found = [(tuple(range(OWN - lent.get(me, 0))), me, ())]
    taken = lent.get(mirrored(me), 0)
    if taken:
        found.append((tuple(range(UNITS - taken, UNITS)), mirrored(me), ()))
    return found


def source_lists():
    everyone = range(BLOCKS)
    return [[sources_of(me, 0, "z", "y")[n] + sources_of(me, 1, "y", "z")[n] for me in everyone] for n in range(3)]


def tables():
    stages = source_lists()
    lent = {}
    for early in range(PLANE):
        late = mirrored(early)
        costs = []
        for units in range(LENT + 1):
            cost = []
            for me in (early, late):
                lines = [make_table([stage[me]], [wants(me, {late: units})]) for stage in stages]
                cost.append(sum(int(line[0, 0]) + 1.3 * int(line[0, 1]) for line in lines))
            costs.append((max(cost) + 0.01 * units, units))
        lent[late] = min(costs)[1]
    return [make_table(stage, [wants(me, lent) for me in range(BLOCKS)]) for stage in stages], lent


def shards(stream_one, stream_two, stream_value, short_stream_taps, medium_filter, residual, norm_gain, queries, keys, values):
    rows, width = stream_one.shape
    middle = queries.shape[1] // 2
    me = lax.axis_index("ctx")
    own, given = pack_call(keys, values, queries)
    other = moved(own, x=1)
    (near, far, across), lent = tables()
    lenders = [i for i in range(BLOCKS) if lent.get(i, 0)]
    given = lax.ppermute(given, "ctx", [(i, mirrored(i)) for i in lenders])
    a = near_line(own, own, "z")
    b = near_line(other, other, "y")
    a, b, given = lax.optimization_barrier((a, b, given))
    a_line, b_line = jnp.stack(a), jnp.stack(b)
    lines = [moved(a_line, y=1), moved(a_line, y=-1), moved(b_line, z=1), moved(b_line, z=-1)]
    tail = tail_call(stream_one, stream_two, stream_value, short_stream_taps)
    halo = lax.ppermute(tail, "ctx", [(i, i + 1) for i in range(BLOCKS - 1)])
    turned = [turn_call(queries), turn_call(given)]
    states = attend_call(near, [part[None] for part in a + b], turned, [None, None])
    a_line, b_line, states = lax.optimization_barrier((a_line, b_line, states))
    crossed = [moved(a_line, y=2), moved(b_line, z=2)]
    states = attend_call(far, lines, turned, states)
    kept, helped = attend_call(across, crossed, turned, states, last=True)
    returned = lax.ppermute(helped, "ctx", [(mirrored(i), i) for i in lenders])
    halo, helped = lax.optimization_barrier((halo, helped))
    branch, squares = mixer_call(stream_one, stream_two, stream_value, halo, short_stream_taps, reversed_taps(medium_filter), residual)
    sums = squares.reshape(rows)
    sums, returned = lax.optimization_barrier((sums, returned))
    parts = [lax.ppermute(sums, "tp", [(i, i ^ step) for i in range(4)]) for step in (1, 2, 3)]
    bound = jnp.array([OWN - lent.get(i, 0) for i in range(BLOCKS)], jnp.int32)[me] * (UNIT * HD) - middle
    later = jnp.where(lax.broadcasted_iota(jnp.int32, returned.shape, 1) >= bound, returned, kept[:, middle:])
    attended = jnp.concatenate([kept[:, :middle], later], axis=1)
    scaling = lax.rsqrt((sums + parts[0] + parts[1] + parts[2]) / D + 1e-06)
    normed = (branch * scaling[:, None] * norm_gain.astype(f32)[None, :]).astype(bf)
    return normed, attended


def solution(mesh):
    in_specs = (P("ctx", "tp"), P("ctx", "tp"), P("ctx", "tp"), P(None, None, "tp"), P("tp", None),
                P("ctx", "tp"), P("tp"), P("ctx", "tp"), P("ctx", "tp"), P("ctx", "tp"))
    return jax.shard_map(shards, mesh=mesh, in_specs=in_specs, out_specs=(P("ctx", "tp"), P("ctx", "tp")), check_vma=False)
```

```python
import functools
import math

import jax
import jax.numpy as jnp
import numpy as np
from jax import lax
from jax.experimental import pallas as pl
from jax.experimental.pallas import tpu as pltpu
from jax.sharding import PartitionSpec as P

f32=jnp.float32; bf=jnp.bfloat16
SHORT=7; GROUP=16; LANES=128; EDGE=16; TAPS=128; BLK=64
VMEM = 60 * 2**20
ATTEND_VMEM = 28 * 2**20
MIXER_VMEM = 60 * 2**20
LIGHT = pl.CostEstimate(flops=1000, bytes_accessed=1000, transcendentals=0)
PARAMS = pltpu.CompilerParams(vmem_limit_bytes=VMEM)

def tail_kernel(one, two, val, taps, out, streams, x_scr, sems):
    keep = TAPS
    first = one.shape[0] - keep - EDGE
    copies = [pltpu.make_async_copy(ref.at[first:], streams.at[n], sems.at[n]) for n, ref in enumerate((one, val, two))]
    for copy in copies:
        copy.start()
    for copy in copies:
        copy.wait()
    for lanes in range(one.shape[1] // LANES):
        c = slice(lanes * LANES, (lanes + 1) * LANES)
        t = taps[:, :, c].astype(f32)

        def short(stream, which, slot):
            x_scr[slot] = streams[stream, :, c].astype(f32)
            total = t[which, 0:1] * x_scr[slot, EDGE:EDGE + keep, :]
            for j in range(1, SHORT):
                total += t[which, j:j + 1] * x_scr[slot, EDGE - j:EDGE - j + keep, :]
            return total
        slot = 2 * (lanes % 4)
        out[0:keep, c] = (short(0, 0, slot) * short(1, 2, slot + 1)).astype(bf)
    for n, stream in enumerate((0, 2, 1)):
        out[keep + EDGE * n:keep + EDGE * (n + 1)] = streams[stream, keep:]


def tail_call(one, two, val, taps):
    rows, width = one.shape
    hbm = pl.BlockSpec(memory_space=pltpu.HBM)
    vmem = pl.BlockSpec(memory_space=pltpu.VMEM)
    return pl.pallas_call(tail_kernel, in_specs=[hbm] * 3 + [vmem], out_specs=vmem,
        out_shape=jax.ShapeDtypeStruct((TAPS + 3 * EDGE, width), bf),
        scratch_shapes=[pltpu.VMEM((3, TAPS + EDGE, width), bf), pltpu.VMEM((8, TAPS + EDGE, LANES), f32),
                        pltpu.SemaphoreType.DMA((3,))],
        compiler_params=pltpu.CompilerParams(vmem_limit_bytes=ATTEND_VMEM),
        cost_estimate=LIGHT,
        name="mixed_tail")(one, two, val, taps)


def mixer_kernel(one, two, val, halo, taps, filters, res, branch, sums, squares, x_scr, m_scr, t_scr):
    rows = one.shape[0]
    groups = LANES // GROUP
    span = BLK + TAPS
    lane = lax.broadcasted_iota(jnp.int32, (BLK, LANES), 1) // GROUP
    flip = (lax.broadcasted_iota(jnp.int32, (TAPS, 2 * TAPS), 0) + lax.broadcasted_iota(jnp.int32, (TAPS, 2 * TAPS), 1)) == TAPS
    rev = jnp.dot(filters[...], jnp.where(flip, 1.0, 0.0).astype(bf), preferred_element_type=f32)
    for unit in range(one.shape[1] // LANES):
        lanes = slice(unit * LANES, (unit + 1) * LANES)
        t = taps[:, :, lanes].astype(f32)

        def short(ref, n):
            lo = TAPS + EDGE * n
            x_scr[unit, n, 0:EDGE] = halo[lo:lo + EDGE, lanes].astype(f32)
            x_scr[unit, n, EDGE:] = ref[:, lanes].astype(f32)
            total = t[n, 0:1] * x_scr[unit, n, EDGE:, :]
            for j in range(1, SHORT):
                total += t[n, j:j + 1] * x_scr[unit, n, EDGE - j:EDGE - j + rows, :]
            return total
        m_scr[unit, 0:TAPS] = halo[0:TAPS, lanes]
        m_scr[unit, TAPS:] = (short(one, 0) * short(val, 2)).astype(bf)
        gate = short(two, 1)
        for g in range(groups):
            row = jnp.broadcast_to(rev[unit * groups + g:unit * groups + g + 1, :], (BLK, 2 * TAPS))
            rolled = pltpu.roll(row, 0, 1, stride=1, stride_axis=0)
            t_scr[unit, g * BLK:(g + 1) * BLK] = rolled.astype(bf)
        for pair in range(rows // (2 * BLK)):
            at = 2 * BLK * pair
            window = jnp.concatenate([m_scr[unit, at:at + span], m_scr[unit, at + BLK:at + BLK + span]], axis=1)
            wide = jnp.dot(t_scr[unit, :, :span], window, preferred_element_type=f32)
            for half in range(2):
                r = slice(at + BLK * half, at + BLK * (half + 1))
                c = slice(LANES * half, LANES * (half + 1))
                medium = wide[0:BLK, c]
                for g in range(1, groups):
                    medium = jnp.where(lane == g, wide[g * BLK:(g + 1) * BLK, c], medium)
                summed = res[r, lanes].astype(f32) + gate[r] * medium
                branch[r, lanes] = summed
                square = summed * summed
                if unit == 0:
                    square += jnp.where(pl.program_id(0) == 0, 0.0, squares[r])
                else:
                    square += squares[r]
                squares[r] = square

    @pl.when(pl.program_id(0) == pl.num_programs(0) - 1)
    def _():
        sums[...] = jnp.sum(squares[...].T, axis=0, keepdims=True)


def mixer_call(one, two, val, halo, taps, filters, res):
    rows, width = one.shape
    units = 4
    tile = units * LANES
    groups = tile // GROUP
    spec = pl.BlockSpec((rows, tile), lambda i: (0, i))
    return pl.pallas_call(mixer_kernel, grid=(width // tile,),
        in_specs=[spec] * 3 + [pl.BlockSpec((halo.shape[0], tile), lambda i: (0, i)),
            pl.BlockSpec((3, SHORT, tile), lambda i: (0, 0, i)),
            pl.BlockSpec((groups, TAPS), lambda i: (i, 0)), spec],
        out_specs=[spec, pl.BlockSpec((1, rows), lambda i: (0, 0))],
        out_shape=[jax.ShapeDtypeStruct((rows, width), f32), jax.ShapeDtypeStruct((1, rows), f32)],
        scratch_shapes=[pltpu.VMEM((rows, LANES), f32), pltpu.VMEM((units, 3, EDGE + rows, LANES), f32), pltpu.VMEM((units, TAPS + rows, LANES), bf),
            pltpu.VMEM((units, LANES // GROUP * BLK, 2 * TAPS), bf)],
        compiler_params=pltpu.CompilerParams(vmem_limit_bytes=MIXER_VMEM),
        cost_estimate=LIGHT,
        name="mixer")(one, two, val, halo, taps, filters, res)


HD = 128
UNIT = 2
OWN, LENT = 4, 2
UNITS = OWN + LENT
UNROLL = 4
ONES = 16
EMPTY, FULL, DIAGONAL = 0, 1, 2
DUMMIES = 3
SCALE = math.log2(math.e) / math.sqrt(HD)


def pack_kernel(keys, values, queries, packed, given):
    packed[:, :HD] = keys[...]
    turned = values[...].astype(f32).T.astype(bf)
    for part in range(values.shape[0] // HD):
        packed[part * HD:(part + 1) * HD, HD:] = turned[:, part * HD:(part + 1) * HD]
    given[...] = queries[...]


def pack_call(keys, values, queries):
    rows, width = queries.shape
    shape = (rows, width // 2)
    whole = lambda i: (0, 0)
    return pl.pallas_call(pack_kernel, grid=(1,),
        in_specs=[pl.BlockSpec(keys.shape, whole), pl.BlockSpec(values.shape, whole), pl.BlockSpec(shape, lambda i: (0, 1))],
        out_specs=[pl.BlockSpec((rows, 2 * HD), whole), pl.BlockSpec(shape, whole)],
        out_shape=[jax.ShapeDtypeStruct((rows, 2 * HD), bf), jax.ShapeDtypeStruct(shape, bf)],
        compiler_params=PARAMS, cost_estimate=LIGHT, name="pack_keys")(keys, values, queries)


def turn_kernel(queries, turned):
    rows = queries.shape[0]
    for head in range(UNIT):
        wide = queries[:, head * HD:(head + 1) * HD].astype(f32).T * SCALE
        high = wide.astype(bf)
        columns = slice(head * rows, (head + 1) * rows)
        turned[0, :HD, columns] = high
        turned[0, HD:, columns] = (wide - high.astype(f32)).astype(bf)


def turn_call(queries):
    rows, width = queries.shape
    units = width // (UNIT * HD)
    return pl.pallas_call(turn_kernel, grid=(units,),
        in_specs=[pl.BlockSpec((rows, UNIT * HD), lambda i: (0, i))],
        out_specs=pl.BlockSpec((1, 2 * HD, UNIT * rows), lambda i: (i, 0, 0)),
        out_shape=jax.ShapeDtypeStruct((units, 2 * HD, UNIT * rows), bf),
        compiler_params=pltpu.CompilerParams(vmem_limit_bytes=ATTEND_VMEM), cost_estimate=LIGHT,
        name="turn_queries")(queries)


def table_layout(shards):
    slots = shards + DUMMIES + (shards + DUMMIES) % 2
    at_a = 2 + DUMMIES
    at_b = at_a + shards
    at_live = at_b + shards
    at_fast = at_live + slots
    at_slow = at_fast + UNITS * (slots // 2)
    return slots, at_a, at_b, at_live, at_fast, at_slow, at_slow + UNITS * (slots // 2)


def attend_kernel(sizes, groups, starts, last, rows, *refs):
    refs = list(refs)
    take = lambda n: [refs.pop(0) for _ in range(n)]
    table, = take(1)
    pieces = take(len(sizes))
    q_in = take(len(groups))
    state_in = [None if start else take(2) for start in starts]
    results = take(len(groups)) if last else [take(2) for _ in groups]
    q, kv, acc, top, s_scr, p_scr, a_scr, load_sem, kv_sem, store_sem = refs
    shards = sum(sizes)
    slots, at_a, at_b, at_live, at_fast, at_slow, _ = table_layout(shards)
    me = lax.axis_index("ctx")
    n_fast = table[me, 0]
    n_slow = table[me, 1]
    half = 2 * rows
    parts = rows // HD

    copies = []
    number = 0
    for piece, size in zip(pieces, sizes):
        for index in range(size):
            for n, at in enumerate((at_a, at_b)):
                slot = table[me, at + number]
                copies.append((slot, pltpu.make_async_copy(
                    piece.at[index], kv.at[jnp.maximum(slot, 0)], kv_sem.at[2 * number + n])))
            number += 1
    for slot, copy in copies:
        pl.when(slot >= 0)(copy.start)
    loads = []
    at = 0
    for n, count in enumerate(groups):
        group = pl.ds(at, count)
        loads.append(pltpu.make_async_copy(q_in[n], q.at[group], load_sem.at[3 * n]))
        if not starts[n]:
            loads.append(pltpu.make_async_copy(state_in[n][0], acc.at[group], load_sem.at[3 * n + 1]))
            loads.append(pltpu.make_async_copy(state_in[n][1], top.at[group], load_sem.at[3 * n + 2]))
        at += count
    for copy in loads:
        copy.start()
    at = 0
    for n, count in enumerate(groups):
        if starts[n]:
            for unit in range(at, at + count):
                acc[unit] = jnp.zeros(acc.shape[1:], f32)
                top[unit] = jnp.full(top.shape[1:], -1e30, f32)
        at += count
    for slot, copy in copies:
        pl.when(slot >= 0)(copy.wait)
    for copy in loads:
        copy.wait()
    for n in range(DUMMIES):
        slot = table[me, 2 + n]

        @pl.when(slot >= 0)
        def _():
            kv[slot, :, HD:] = jnp.zeros((rows, HD), bf)

    def decode(code):
        return code % 8, (code // 8) % 64, (code // 512) % 4, (code // 2048) % 4

    def multiply_keys(unit, block):
        k = jnp.concatenate([kv[2 * block, :, :HD], kv[2 * block + 1, :, :HD]], axis=0)
        k = jnp.concatenate([k, k], axis=1)
        return jnp.dot(k, q[unit], preferred_element_type=f32)

    def multiply_values(unit, block, weights, factor):
        v = jnp.concatenate([kv[2 * block + n // parts, (n % parts) * HD:(n % parts + 1) * HD, HD:]
                             for n in range(2 * parts)], axis=1)
        live = [jnp.full((ONES, rows), table[me, at_live + 2 * block + n].astype(f32)).astype(bf) for n in range(2)]
        v = jnp.concatenate([v, jnp.concatenate(live, axis=1)], axis=0)
        acc[unit] = acc[unit] * factor + jnp.dot(v, weights, preferred_element_type=f32)

    def soften(unit, s):
        old = top[unit, 0:1]
        new = jnp.maximum(old, jnp.max(s, axis=0, keepdims=True))
        top[unit, 0:1] = new
        return jnp.exp2(s - new).astype(bf), jnp.exp2(old - new)

    def masked_step(number):
        unit, block, *modes = decode(table[me, at_slow + number])
        lead = lax.broadcasted_iota(jnp.int32, (rows, rows), 0) - lax.broadcasted_iota(jnp.int32, (rows, rows), 1)
        lead = jnp.concatenate([lead, lead], axis=1)
        limits = [jnp.where(mode == FULL, rows, jnp.where(mode == DIAGONAL, 0, -2 * rows)) for mode in modes]
        s = multiply_keys(unit, block)
        s = jnp.concatenate([jnp.where(lead <= limits[n], s[n * rows:(n + 1) * rows], -1e30) for n in range(2)], axis=0)
        weights, factor = soften(unit, s)
        return unit, block, weights, factor

    @pl.loop(0, n_slow // 2)
    def _(step):
        one = masked_step(2 * step)
        two = masked_step(2 * step + 1)
        multiply_values(*one)
        multiply_values(*two)

    @pl.when(n_slow % 2 == 1)
    def _():
        multiply_values(*masked_step(n_slow - 1))

    def fast_entry(number):
        return decode(table[me, at_fast + jnp.clip(number, 0, n_fast - 1)])[:2]

    def region(number, unroll):
        todo = [fast_entry(number + n) for n in range(unroll + 1)]
        s = s_scr[...]
        pending = (*fast_entry(number - 1), p_scr[...], a_scr[0:1])
        for (unit, block), later in zip(todo, todo[1:]):
            coming = multiply_keys(*later)
            multiply_values(*pending)
            weights, factor = soften(unit, s)
            pending = (unit, block, weights, factor)
            s = coming
        s_scr[...] = s
        p_scr[...] = pending[2]
        a_scr[0:1] = pending[3]

    @pl.when(n_fast > 0)
    def _():
        s_scr[...] = multiply_keys(*fast_entry(0))
        p_scr[...] = jnp.zeros_like(p_scr)
        a_scr[...] = jnp.ones_like(a_scr)

        @pl.loop(0, n_fast // UNROLL)
        def _(step):
            region(UNROLL * step, UNROLL)

        @pl.when((n_fast // 2) % 2 == 1)
        def _():
            region(n_fast // UNROLL * UNROLL, 2)

        @pl.when(n_fast % 2 == 1)
        def _():
            region(n_fast - 1, 1)

        multiply_values(*fast_entry(n_fast - 1), p_scr[...], a_scr[0:1])

    if last:
        at = 0
        for n, count in enumerate(groups):
            for unit in range(count):
                for head in range(UNIT):
                    c = slice(head * rows, (head + 1) * rows)
                    value = acc[at + unit, :HD, c] * (1.0 / acc[at + unit, HD:HD + 1, c])
                    to = (unit * UNIT + head) * HD
                    results[n][:, to:to + HD] = value.T.astype(bf)
            at += count
    else:
        stores = []
        at = 0
        for n, count in enumerate(groups):
            group = pl.ds(at, count)
            stores.append(pltpu.make_async_copy(acc.at[group], results[n][0], store_sem.at[2 * n]))
            stores.append(pltpu.make_async_copy(top.at[group], results[n][1], store_sem.at[2 * n + 1]))
            at += count
        for copy in stores:
            copy.start()
        for copy in stores:
            copy.wait()


def attend_call(table, pieces, turned, states, last=False):
    wide = turned[0].shape[2]
    rows = wide // UNIT
    sizes = tuple(piece.shape[0] for piece in pieces)
    shards = sum(sizes)
    slots = table_layout(shards)[0]
    groups = tuple(t.shape[0] for t in turned)
    units = sum(groups)
    starts = tuple(state is None for state in states)
    hbm = pl.BlockSpec(memory_space=pltpu.HBM)
    anywhere = pl.BlockSpec(memory_space=pl.ANY)
    operands = [table, *pieces, *turned] + [part for state in states if state is not None for part in state]
    if last:
        out_shape = [jax.ShapeDtypeStruct((rows, count * UNIT * HD), bf) for count in groups]
        out_specs = [pl.BlockSpec(memory_space=pltpu.VMEM)] * len(groups)
    else:
        out_shape = []
        for count in groups:
            out_shape.append(jax.ShapeDtypeStruct((count, HD + ONES, wide), f32))
            out_shape.append(jax.ShapeDtypeStruct((count, 8, wide), f32))
        out_specs = [hbm] * len(out_shape)
    result = pl.pallas_call(
        functools.partial(attend_kernel, sizes, groups, starts, last, rows),
        in_specs=[pl.BlockSpec(memory_space=pltpu.SMEM)] + [anywhere] * len(pieces) + [hbm] * (len(operands) - 1 - len(pieces)),
        out_specs=out_specs,
        out_shape=out_shape,
        scratch_shapes=[
            pltpu.VMEM((units, 2 * HD, wide), bf),
            pltpu.VMEM((slots, rows, 2 * HD), bf),
            pltpu.VMEM((units, HD + ONES, wide), f32),
            pltpu.VMEM((units, 8, wide), f32),
            pltpu.VMEM((2 * rows, 2 * rows), f32),
            pltpu.VMEM((2 * rows, 2 * rows), bf),
            pltpu.VMEM((8, 2 * rows), f32),
            pltpu.SemaphoreType.DMA((3 * len(groups),)),
            pltpu.SemaphoreType.DMA((2 * shards,)),
            pltpu.SemaphoreType.DMA((2 * len(groups),)),
        ],
        compiler_params=pltpu.CompilerParams(vmem_limit_bytes=ATTEND_VMEM),
        cost_estimate=LIGHT,
        name="attend",
    )(*operands)
    if last:
        return list(result)
    return [tuple(result[2 * n:2 * n + 2]) for n in range(len(groups))]


def make_table(sources_of, wants_of):
    lines = []
    for sources, wanted in zip(sources_of, wants_of):
        shards = len(sources)
        slots, at_a, at_b, at_live, at_fast, at_slow, size = table_layout(shards)
        line = np.zeros(size, np.int32)
        line[2:at_live] = -1
        line[at_live:at_fast] = 1
        fast, slow, dummies = [], [], []
        used = 0

        def place(members):
            nonlocal used
            modes = []
            for shard, mode in members:
                line[at_a + shard] = used
                used += 1
                modes.append(mode)
            if len(members) % 2:
                line[at_b + members[-1][0]] = used
                line[at_live + used] = 0
                dummies.append(used)
                used += 1
                modes.append(FULL if members[-1][1] == FULL else EMPTY)
            return [((used - len(modes)) // 2 + n, modes[2 * n], modes[2 * n + 1]) for n in range(len(modes) // 2)]

        shared = []
        placed = set()
        for units, position, skipped in wanted:
            new = [(n, FULL if source < position else DIAGONAL) for n, source in enumerate(sources)
                   if source <= position and source not in skipped and n not in placed]
            new.sort(key=lambda member: member[1])
            blocks = place(new)
            placed.update(n for n, _ in new)
            for unit in units:
                for block, one, two in shared + blocks:
                    code = unit + 8 * block
                    if (one, two) == (FULL, FULL):
                        fast.append(code)
                    else:
                        slow.append(code + 512 * one + 2048 * two)
            shared = shared + [(block, FULL, FULL) for block, _, _ in blocks]
        assert used <= slots and len(dummies) <= DUMMIES
        line[0], line[1] = len(fast), len(slow)
        line[2:2 + len(dummies)] = dummies
        line[at_fast:at_fast + len(fast)] = fast
        line[at_slow:at_slow + len(slow)] = slow
        lines.append(line)
    return np.array(lines)


D = 8192
Z = Y = 4
PLANE = Z * Y
BLOCKS = 2 * PLANE


def neighbour(i, x=0, z=0, y=0):
    at_x, at_z, at_y = i // PLANE, (i // Y) % Z, i % Y
    return (at_x + x) % 2 * PLANE + (at_z + z) % Z * Y + (at_y + y) % Y


def mirrored(i):
    return BLOCKS - 1 - i


def moved(value, x=0, z=0, y=0):
    return lax.ppermute(value, "ctx", [(i, neighbour(i, x, z, y)) for i in range(BLOCKS)])


def near_line(first, last, axis):
    return [first, moved(first, **{axis: 1}), moved(first, **{axis: -1}), moved(last, **{axis: 2})]


def sources_of(me, plane, axis, other):
    base = neighbour(me, x=plane)
    line = [neighbour(base, **{axis: -step}) for step in (0, 1, -1, 2)]
    lines = [[neighbour(b, **{other: -step}) for b in line] for step in (1, -1, 2)]
    return [base] + line[1:], lines[0] + lines[1], lines[2]


def source_lists():
    everyone = range(BLOCKS)
    near, far, across = [[sources_of(me, 0, "z", "y")[n] + sources_of(me, 1, "y", "z")[n] for me in everyone]
                         for n in range(3)]
    return near, [one + two for one, two in zip(far, near)], across


def wants(me, lent, stage, near):
    found = [(tuple(range(OWN - lent.get(me, 0))), me, near if stage == 1 else ())]
    taken = lent.get(mirrored(me), 0)
    if taken and stage > 0:
        found.append((tuple(range(UNITS - taken, UNITS)), mirrored(me), ()))
    return found


def tables():
    stages = source_lists()
    lent = {}
    for early in range(PLANE):
        late = mirrored(early)
        costs = []
        for units in range(LENT + 1):
            cost = []
            for me in (early, late):
                lines = [make_table([stage[me]], [wants(me, {late: units}, n, tuple(stages[0][me]))])
                         for n, stage in enumerate(stages)]
                cost.append(sum(int(line[0, 0]) + 1.3 * int(line[0, 1]) for line in lines))
            costs.append((max(cost) + 0.01 * units, units))
        lent[late] = min(costs)[1]
    return [make_table(stage, [wants(me, lent, n, tuple(stages[0][me])) for me in range(BLOCKS)])
            for n, stage in enumerate(stages)], lent


def shards(stream_one, stream_two, stream_value, short_stream_taps, medium_filter, residual, norm_gain, queries, keys, values):
    rows, width = stream_one.shape
    middle = queries.shape[1] // 2
    me = lax.axis_index("ctx")
    own, given = pack_call(keys, values, queries)
    other = moved(own, x=1)
    (near, far, across), lent = tables()
    lenders = [i for i in range(BLOCKS) if lent.get(i, 0)]
    a = near_line(own, own, "z")
    b = near_line(other, other, "y")
    a, b = lax.optimization_barrier((a, b))
    a_line, b_line, given = lax.optimization_barrier((jnp.stack(a), jnp.stack(b), given))
    given = lax.ppermute(given, "ctx", [(i, mirrored(i)) for i in lenders])
    lines = [moved(a_line, y=1), moved(a_line, y=-1), moved(b_line, z=1), moved(b_line, z=-1)]
    tail = tail_call(stream_one, stream_two, stream_value, short_stream_taps)
    halo = lax.ppermute(tail, "ctx", [(i, i + 1) for i in range(BLOCKS - 1)])
    turned = [turn_call(queries), turn_call(given)]
    start = [part[None] for part in a + b]
    state, = attend_call(near, start, turned[:1], [None])
    a_line, b_line, state = lax.optimization_barrier((a_line, b_line, state))
    crossed = [moved(a_line, y=2), moved(b_line, z=2)]
    states = attend_call(far, lines + start, turned, [state, None])
    kept, helped = attend_call(across, crossed, turned, states, last=True)
    returned = lax.ppermute(helped, "ctx", [(mirrored(i), i) for i in lenders])
    halo, helped = lax.optimization_barrier((halo, helped))
    branch, squares = mixer_call(stream_one, stream_two, stream_value, halo, short_stream_taps, medium_filter, residual)
    sums = squares
    sums, returned = lax.optimization_barrier((sums, returned))
    parts = [lax.ppermute(sums, "tp", [(i, i ^ step) for i in range(4)]) for step in (1, 2, 3)]
    least = [min(i for i in lenders if lent[i] > level) for level in range(LENT)]
    assert all(lent[i] == sum(i >= bound for bound in least) for i in lent)
    count = sum((me >= bound).astype(jnp.int32) for bound in least)
    bound = (OWN - count) * (UNIT * HD) - middle
    later = jnp.where(lax.broadcasted_iota(jnp.int32, returned.shape, 1) >= bound, returned, kept[:, middle:])
    attended = jnp.concatenate([kept[:, :middle], later], axis=1)
    scaling = lax.rsqrt((sums + parts[0] + parts[1] + parts[2]) / D + 1e-06)
    normed = (branch * scaling.reshape(rows, 1) * norm_gain.astype(f32)[None, :]).astype(bf)
    return normed, attended


def solution(mesh):
    in_specs = (P("ctx", "tp"), P("ctx", "tp"), P("ctx", "tp"), P(None, None, "tp"), P("tp", None),
                P("ctx", "tp"), P("tp"), P("ctx", "tp"), P("ctx", "tp"), P("ctx", "tp"))
    return jax.shard_map(shards, mesh=mesh, in_specs=in_specs, out_specs=(P("ctx", "tp"), P("ctx", "tp")), check_vma=False)
```

```python
import functools
import math

import jax
import jax.numpy as jnp
import numpy as np
from jax import lax
from jax.experimental import pallas as pl
from jax.experimental.pallas import tpu as pltpu
from jax.sharding import PartitionSpec as P

f32=jnp.float32; bf=jnp.bfloat16
SHORT=7; GROUP=16; LANES=128; EDGE=16; TAPS=128; BLK=64
VMEM = 60 * 2**20
ATTEND_VMEM = 28 * 2**20
LIGHT = pl.CostEstimate(flops=1000, bytes_accessed=1000, transcendentals=0)
PARAMS = pltpu.CompilerParams(vmem_limit_bytes=VMEM)

def tail_kernel(one, two, val, taps, out, streams, x_scr, sems):
    keep = TAPS
    first = one.shape[0] - keep - EDGE
    copies = [pltpu.make_async_copy(ref.at[first:], streams.at[n], sems.at[n]) for n, ref in enumerate((one, val, two))]
    for copy in copies:
        copy.start()
    for copy in copies:
        copy.wait()
    for lanes in range(one.shape[1] // LANES):
        c = slice(lanes * LANES, (lanes + 1) * LANES)
        t = taps[:, :, c].astype(f32)

        def short(stream, which, slot):
            x_scr[slot] = streams[stream, :, c].astype(f32)
            total = t[which, 0:1] * x_scr[slot, EDGE:EDGE + keep, :]
            for j in range(1, SHORT):
                total += t[which, j:j + 1] * x_scr[slot, EDGE - j:EDGE - j + keep, :]
            return total
        slot = 2 * (lanes % 4)
        out[0:keep, c] = (short(0, 0, slot) * short(1, 2, slot + 1)).astype(bf)
    for n, stream in enumerate((0, 2, 1)):
        out[keep + EDGE * n:keep + EDGE * (n + 1)] = streams[stream, keep:]


def tail_call(one, two, val, taps):
    rows, width = one.shape
    hbm = pl.BlockSpec(memory_space=pltpu.HBM)
    vmem = pl.BlockSpec(memory_space=pltpu.VMEM)
    return pl.pallas_call(tail_kernel, in_specs=[hbm] * 3 + [vmem], out_specs=vmem,
        out_shape=jax.ShapeDtypeStruct((TAPS + 3 * EDGE, width), bf),
        scratch_shapes=[pltpu.VMEM((3, TAPS + EDGE, width), bf), pltpu.VMEM((8, TAPS + EDGE, LANES), f32),
                        pltpu.SemaphoreType.DMA((3,))],
        compiler_params=pltpu.CompilerParams(vmem_limit_bytes=ATTEND_VMEM),
        cost_estimate=LIGHT,
        name="mixed_tail")(one, two, val, taps)


def mixer_kernel(one, two, val, halo, taps, rev, res, branch, sums, squares, x_scr, m_scr, t_scr):
    rows = one.shape[0]
    groups = LANES // GROUP
    span = BLK + TAPS
    lane = lax.broadcasted_iota(jnp.int32, (BLK, LANES), 1) // GROUP
    for unit in range(one.shape[1] // LANES):
        lanes = slice(unit * LANES, (unit + 1) * LANES)
        t = taps[:, :, lanes].astype(f32)

        def short(ref, n):
            lo = TAPS + EDGE * n
            x_scr[unit, n, 0:EDGE] = halo[lo:lo + EDGE, lanes].astype(f32)
            x_scr[unit, n, EDGE:] = ref[:, lanes].astype(f32)
            total = t[n, 0:1] * x_scr[unit, n, EDGE:, :]
            for j in range(1, SHORT):
                total += t[n, j:j + 1] * x_scr[unit, n, EDGE - j:EDGE - j + rows, :]
            return total
        m_scr[unit, 0:TAPS] = halo[0:TAPS, lanes]
        m_scr[unit, TAPS:] = (short(one, 0) * short(val, 2)).astype(bf)
        gate = short(two, 1)
        for g in range(groups):
            row = jnp.broadcast_to(rev[unit * groups + g:unit * groups + g + 1, :], (BLK, 2 * TAPS))
            rolled = pltpu.roll(row, 0, 1, stride=1, stride_axis=0)
            t_scr[unit, g * BLK:(g + 1) * BLK] = rolled.astype(bf)
        for pair in range(rows // (2 * BLK)):
            at = 2 * BLK * pair
            window = jnp.concatenate([m_scr[unit, at:at + span], m_scr[unit, at + BLK:at + BLK + span]], axis=1)
            wide = jnp.dot(t_scr[unit, :, :span], window, preferred_element_type=f32)
            for half in range(2):
                r = slice(at + BLK * half, at + BLK * (half + 1))
                c = slice(LANES * half, LANES * (half + 1))
                medium = wide[0:BLK, c]
                for g in range(1, groups):
                    medium = jnp.where(lane == g, wide[g * BLK:(g + 1) * BLK, c], medium)
                summed = res[r, lanes].astype(f32) + gate[r] * medium
                branch[r, lanes] = summed
                square = summed * summed
                if unit == 0:
                    square += jnp.where(pl.program_id(0) == 0, 0.0, squares[r])
                else:
                    square += squares[r]
                squares[r] = square

    @pl.when(pl.program_id(0) == pl.num_programs(0) - 1)
    def _():
        sums[...] = jnp.sum(squares[...].T, axis=0, keepdims=True)


def mixer_call(one, two, val, halo, taps, rev, res):
    rows, width = one.shape
    units = 4
    tile = units * LANES
    groups = tile // GROUP
    spec = pl.BlockSpec((rows, tile), lambda i: (0, i))
    return pl.pallas_call(mixer_kernel, grid=(width // tile,),
        in_specs=[spec] * 3 + [pl.BlockSpec((halo.shape[0], tile), lambda i: (0, i)),
            pl.BlockSpec((3, SHORT, tile), lambda i: (0, 0, i)),
            pl.BlockSpec((groups, 2 * TAPS), lambda i: (i, 0)), spec],
        out_specs=[spec, pl.BlockSpec((1, rows), lambda i: (0, 0))],
        out_shape=[jax.ShapeDtypeStruct((rows, width), f32), jax.ShapeDtypeStruct((1, rows), f32)],
        scratch_shapes=[pltpu.VMEM((rows, LANES), f32), pltpu.VMEM((units, 3, EDGE + rows, LANES), f32), pltpu.VMEM((units, TAPS + rows, LANES), bf),
            pltpu.VMEM((units, LANES // GROUP * BLK, 2 * TAPS), bf)],
        compiler_params=PARAMS,
        cost_estimate=LIGHT,
        name="mixer")(one, two, val, halo, taps, rev, res)


def reversed_taps(filters):
    flipped = filters.astype(f32)[:, ::-1]
    return jnp.pad(flipped, ((0, 0), (1, TAPS - 1)))


HD = 128
UNIT = 2
OWN, LENT = 4, 2
UNITS = OWN + LENT
UNROLL = 4
ONES = 16
EMPTY, FULL, DIAGONAL = 0, 1, 2
DUMMIES = 3
SCALE = math.log2(math.e) / math.sqrt(HD)


def pack_kernel(keys, values, queries, packed, given):
    packed[:, :HD] = keys[...]
    turned = values[...].astype(f32).T.astype(bf)
    for part in range(values.shape[0] // HD):
        packed[part * HD:(part + 1) * HD, HD:] = turned[:, part * HD:(part + 1) * HD]
    given[...] = queries[...]


def pack_call(keys, values, queries):
    rows, width = queries.shape
    shape = (rows, width // 2)
    whole = lambda i: (0, 0)
    return pl.pallas_call(pack_kernel, grid=(1,),
        in_specs=[pl.BlockSpec(keys.shape, whole), pl.BlockSpec(values.shape, whole), pl.BlockSpec(shape, lambda i: (0, 1))],
        out_specs=[pl.BlockSpec((rows, 2 * HD), whole), pl.BlockSpec(shape, whole)],
        out_shape=[jax.ShapeDtypeStruct((rows, 2 * HD), bf), jax.ShapeDtypeStruct(shape, bf)],
        compiler_params=PARAMS, cost_estimate=LIGHT, name="pack_keys")(keys, values, queries)


def turn_kernel(queries, turned):
    rows = queries.shape[0]
    for head in range(UNIT):
        wide = queries[:, head * HD:(head + 1) * HD].astype(f32).T * SCALE
        high = wide.astype(bf)
        columns = slice(head * rows, (head + 1) * rows)
        turned[0, :HD, columns] = high
        turned[0, HD:, columns] = (wide - high.astype(f32)).astype(bf)


def turn_call(queries):
    rows, width = queries.shape
    units = width // (UNIT * HD)
    return pl.pallas_call(turn_kernel, grid=(units,),
        in_specs=[pl.BlockSpec((rows, UNIT * HD), lambda i: (0, i))],
        out_specs=pl.BlockSpec((1, 2 * HD, UNIT * rows), lambda i: (i, 0, 0)),
        out_shape=jax.ShapeDtypeStruct((units, 2 * HD, UNIT * rows), bf),
        compiler_params=pltpu.CompilerParams(vmem_limit_bytes=ATTEND_VMEM), cost_estimate=LIGHT,
        name="turn_queries")(queries)


def table_layout(shards):
    slots = shards + DUMMIES + (shards + DUMMIES) % 2
    at_a = 2 + DUMMIES
    at_b = at_a + shards
    at_live = at_b + shards
    at_fast = at_live + slots
    at_slow = at_fast + UNITS * (slots // 2)
    return slots, at_a, at_b, at_live, at_fast, at_slow, at_slow + UNITS * (slots // 2)


def attend_kernel(sizes, groups, starts, last, rows, *refs):
    refs = list(refs)
    take = lambda n: [refs.pop(0) for _ in range(n)]
    table, = take(1)
    pieces = take(len(sizes))
    q_in = take(len(groups))
    state_in = [None if start else take(2) for start in starts]
    results = take(len(groups)) if last else [take(2) for _ in groups]
    q, kv, acc, top, s_scr, p_scr, a_scr, load_sem, kv_sem, store_sem = refs
    shards = sum(sizes)
    slots, at_a, at_b, at_live, at_fast, at_slow, _ = table_layout(shards)
    me = lax.axis_index("ctx")
    n_fast = table[me, 0]
    n_slow = table[me, 1]
    half = 2 * rows
    parts = rows // HD

    copies = []
    number = 0
    for piece, size in zip(pieces, sizes):
        for index in range(size):
            for n, at in enumerate((at_a, at_b)):
                slot = table[me, at + number]
                copies.append((slot, pltpu.make_async_copy(
                    piece.at[index], kv.at[jnp.maximum(slot, 0)], kv_sem.at[2 * number + n])))
            number += 1
    for slot, copy in copies:
        pl.when(slot >= 0)(copy.start)
    loads = []
    at = 0
    for n, count in enumerate(groups):
        group = pl.ds(at, count)
        loads.append(pltpu.make_async_copy(q_in[n], q.at[group], load_sem.at[3 * n]))
        if not starts[n]:
            loads.append(pltpu.make_async_copy(state_in[n][0], acc.at[group], load_sem.at[3 * n + 1]))
            loads.append(pltpu.make_async_copy(state_in[n][1], top.at[group], load_sem.at[3 * n + 2]))
        at += count
    for copy in loads:
        copy.start()
    at = 0
    for n, count in enumerate(groups):
        if starts[n]:
            for unit in range(at, at + count):
                acc[unit] = jnp.zeros(acc.shape[1:], f32)
                top[unit] = jnp.full(top.shape[1:], -1e30, f32)
        at += count
    for slot, copy in copies:
        pl.when(slot >= 0)(copy.wait)
    for copy in loads:
        copy.wait()
    for n in range(DUMMIES):
        slot = table[me, 2 + n]

        @pl.when(slot >= 0)
        def _():
            kv[slot, :, HD:] = jnp.zeros((rows, HD), bf)

    def decode(code):
        return code % 8, (code // 8) % 64, (code // 512) % 4, (code // 2048) % 4

    def multiply_keys(unit, block):
        k = jnp.concatenate([kv[2 * block, :, :HD], kv[2 * block + 1, :, :HD]], axis=0)
        k = jnp.concatenate([k, k], axis=1)
        return jnp.dot(k, q[unit], preferred_element_type=f32)

    def multiply_values(unit, block, weights, factor):
        v = jnp.concatenate([kv[2 * block + n // parts, (n % parts) * HD:(n % parts + 1) * HD, HD:]
                             for n in range(2 * parts)], axis=1)
        live = [jnp.full((ONES, rows), table[me, at_live + 2 * block + n].astype(f32)).astype(bf) for n in range(2)]
        v = jnp.concatenate([v, jnp.concatenate(live, axis=1)], axis=0)
        acc[unit] = acc[unit] * factor + jnp.dot(v, weights, preferred_element_type=f32)

    def soften(unit, s):
        old = top[unit, 0:1]
        new = jnp.maximum(old, jnp.max(s, axis=0, keepdims=True))
        top[unit, 0:1] = new
        return jnp.exp2(s - new).astype(bf), jnp.exp2(old - new)

    @pl.loop(0, n_slow)
    def _(number):
        unit, block, *modes = decode(table[me, at_slow + number])
        lead = (lax.broadcasted_iota(jnp.int32, (rows, rows), 0) - lax.broadcasted_iota(jnp.int32, (rows, rows), 1))
        lead = jnp.concatenate([lead, lead], axis=1)
        limits = [jnp.where(mode == FULL, rows, jnp.where(mode == DIAGONAL, 0, -2 * rows)) for mode in modes]
        s = multiply_keys(unit, block)
        s = jnp.concatenate([jnp.where(lead <= limits[n], s[n * rows:(n + 1) * rows], -1e30) for n in range(2)], axis=0)
        weights, factor = soften(unit, s)
        multiply_values(unit, block, weights, factor)

    def fast_entry(number):
        return decode(table[me, at_fast + jnp.clip(number, 0, n_fast - 1)])[:2]

    def region(number, unroll):
        todo = [fast_entry(number + n) for n in range(unroll + 1)]
        s = s_scr[...]
        pending = (*fast_entry(number - 1), p_scr[...], a_scr[0:1])
        for (unit, block), later in zip(todo, todo[1:]):
            coming = multiply_keys(*later)
            multiply_values(*pending)
            weights, factor = soften(unit, s)
            pending = (unit, block, weights, factor)
            s = coming
        s_scr[...] = s
        p_scr[...] = pending[2]
        a_scr[0:1] = pending[3]

    @pl.when(n_fast > 0)
    def _():
        s_scr[...] = multiply_keys(*fast_entry(0))
        p_scr[...] = jnp.zeros_like(p_scr)
        a_scr[...] = jnp.ones_like(a_scr)

        @pl.loop(0, n_fast // UNROLL)
        def _(step):
            region(UNROLL * step, UNROLL)

        @pl.when((n_fast // 2) % 2 == 1)
        def _():
            region(n_fast // UNROLL * UNROLL, 2)

        @pl.when(n_fast % 2 == 1)
        def _():
            region(n_fast - 1, 1)

        multiply_values(*fast_entry(n_fast - 1), p_scr[...], a_scr[0:1])

    if last:
        at = 0
        for n, count in enumerate(groups):
            for unit in range(count):
                for head in range(UNIT):
                    c = slice(head * rows, (head + 1) * rows)
                    value = acc[at + unit, :HD, c] * (1.0 / acc[at + unit, HD:HD + 1, c])
                    to = (unit * UNIT + head) * HD
                    results[n][:, to:to + HD] = value.T.astype(bf)
            at += count
    else:
        stores = []
        at = 0
        for n, count in enumerate(groups):
            group = pl.ds(at, count)
            stores.append(pltpu.make_async_copy(acc.at[group], results[n][0], store_sem.at[2 * n]))
            stores.append(pltpu.make_async_copy(top.at[group], results[n][1], store_sem.at[2 * n + 1]))
            at += count
        for copy in stores:
            copy.start()
        for copy in stores:
            copy.wait()


def attend_call(table, pieces, turned, states, last=False):
    wide = turned[0].shape[2]
    rows = wide // UNIT
    sizes = tuple(piece.shape[0] for piece in pieces)
    shards = sum(sizes)
    slots = table_layout(shards)[0]
    groups = tuple(t.shape[0] for t in turned)
    units = sum(groups)
    starts = tuple(state is None for state in states)
    hbm = pl.BlockSpec(memory_space=pltpu.HBM)
    anywhere = pl.BlockSpec(memory_space=pl.ANY)
    operands = [table, *pieces, *turned] + [part for state in states if state is not None for part in state]
    if last:
        out_shape = [jax.ShapeDtypeStruct((rows, count * UNIT * HD), bf) for count in groups]
        out_specs = [pl.BlockSpec(memory_space=pltpu.VMEM)] * len(groups)
    else:
        out_shape = []
        for count in groups:
            out_shape.append(jax.ShapeDtypeStruct((count, HD + ONES, wide), f32))
            out_shape.append(jax.ShapeDtypeStruct((count, 8, wide), f32))
        out_specs = [hbm] * len(out_shape)
    result = pl.pallas_call(
        functools.partial(attend_kernel, sizes, groups, starts, last, rows),
        in_specs=[pl.BlockSpec(memory_space=pltpu.SMEM)] + [anywhere] * len(pieces) + [hbm] * (len(operands) - 1 - len(pieces)),
        out_specs=out_specs,
        out_shape=out_shape,
        scratch_shapes=[
            pltpu.VMEM((units, 2 * HD, wide), bf),
            pltpu.VMEM((slots, rows, 2 * HD), bf),
            pltpu.VMEM((units, HD + ONES, wide), f32),
            pltpu.VMEM((units, 8, wide), f32),
            pltpu.VMEM((2 * rows, 2 * rows), f32),
            pltpu.VMEM((2 * rows, 2 * rows), bf),
            pltpu.VMEM((8, 2 * rows), f32),
            pltpu.SemaphoreType.DMA((3 * len(groups),)),
            pltpu.SemaphoreType.DMA((2 * shards,)),
            pltpu.SemaphoreType.DMA((2 * len(groups),)),
        ],
        compiler_params=pltpu.CompilerParams(vmem_limit_bytes=ATTEND_VMEM),
        cost_estimate=LIGHT,
        name="attend",
    )(*operands)
    if last:
        return list(result)
    return [tuple(result[2 * n:2 * n + 2]) for n in range(len(groups))]


def make_table(sources_of, wants_of):
    lines = []
    for sources, wanted in zip(sources_of, wants_of):
        shards = len(sources)
        slots, at_a, at_b, at_live, at_fast, at_slow, size = table_layout(shards)
        line = np.zeros(size, np.int32)
        line[2:at_live] = -1
        line[at_live:at_fast] = 1
        fast, slow, dummies = [], [], []
        used = 0

        def place(members):
            nonlocal used
            modes = []
            for shard, mode in members:
                line[at_a + shard] = used
                used += 1
                modes.append(mode)
            if len(members) % 2:
                line[at_b + members[-1][0]] = used
                line[at_live + used] = 0
                dummies.append(used)
                used += 1
                modes.append(FULL if members[-1][1] == FULL else EMPTY)
            return [((used - len(modes)) // 2 + n, modes[2 * n], modes[2 * n + 1]) for n in range(len(modes) // 2)]

        shared = []
        placed = set()
        for units, position, skipped in wanted:
            new = [(n, FULL if source < position else DIAGONAL) for n, source in enumerate(sources)
                   if source <= position and source not in skipped and n not in placed]
            new.sort(key=lambda member: member[1])
            blocks = place(new)
            placed.update(n for n, _ in new)
            for unit in units:
                for block, one, two in shared + blocks:
                    code = unit + 8 * block
                    if (one, two) == (FULL, FULL):
                        fast.append(code)
                    else:
                        slow.append(code + 512 * one + 2048 * two)
            shared = shared + [(block, FULL, FULL) for block, _, _ in blocks]
        assert used <= slots and len(dummies) <= DUMMIES
        line[0], line[1] = len(fast), len(slow)
        line[2:2 + len(dummies)] = dummies
        line[at_fast:at_fast + len(fast)] = fast
        line[at_slow:at_slow + len(slow)] = slow
        lines.append(line)
    return np.array(lines)


D = 8192
Z = Y = 4
PLANE = Z * Y
BLOCKS = 2 * PLANE


def neighbour(i, x=0, z=0, y=0):
    at_x, at_z, at_y = i // PLANE, (i // Y) % Z, i % Y
    return (at_x + x) % 2 * PLANE + (at_z + z) % Z * Y + (at_y + y) % Y


def mirrored(i):
    return BLOCKS - 1 - i


def moved(value, x=0, z=0, y=0):
    return lax.ppermute(value, "ctx", [(i, neighbour(i, x, z, y)) for i in range(BLOCKS)])


def near_line(first, last, axis):
    return [first, moved(first, **{axis: 1}), moved(first, **{axis: -1}), moved(last, **{axis: 2})]


def sources_of(me, plane, axis, other):
    base = neighbour(me, x=plane)
    line = [neighbour(base, **{axis: -step}) for step in (0, 1, -1, 2)]
    lines = [[neighbour(b, **{other: -step}) for b in line] for step in (1, -1, 2)]
    return [base] + line[1:], lines[0] + lines[1], lines[2]


def wants(me, lent):
    found = [(tuple(range(OWN - lent.get(me, 0))), me, ())]
    taken = lent.get(mirrored(me), 0)
    if taken:
        found.append((tuple(range(UNITS - taken, UNITS)), mirrored(me), ()))
    return found


def source_lists():
    everyone = range(BLOCKS)
    return [[sources_of(me, 0, "z", "y")[n] + sources_of(me, 1, "y", "z")[n] for me in everyone] for n in range(3)]


def tables():
    stages = source_lists()
    lent = {}
    for early in range(PLANE):
        late = mirrored(early)
        costs = []
        for units in range(LENT + 1):
            cost = []
            for me in (early, late):
                lines = [make_table([stage[me]], [wants(me, {late: units})]) for stage in stages]
                cost.append(sum(int(line[0, 0]) + 1.3 * int(line[0, 1]) for line in lines))
            costs.append((max(cost) + 0.01 * units, units))
        lent[late] = min(costs)[1]
    for late in range(PLANE + 1, BLOCKS):
        lent[late] = max(lent[late], lent[late - 1])
    return [make_table(stage, [wants(me, lent) for me in range(BLOCKS)]) for stage in stages], lent


def shards(stream_one, stream_two, stream_value, short_stream_taps, medium_filter, residual, norm_gain, queries, keys, values):
    rows, width = stream_one.shape
    middle = queries.shape[1] // 2
    me = lax.axis_index("ctx")
    own, given = pack_call(keys, values, queries)
    other = moved(own, x=1)
    (near, far, across), lent = tables()
    lenders = [i for i in range(BLOCKS) if lent.get(i, 0)]
    given = lax.ppermute(given, "ctx", [(i, mirrored(i)) for i in lenders])
    a = near_line(own, own, "z")
    b = near_line(other, other, "y")
    tail = tail_call(stream_one, stream_two, stream_value, short_stream_taps)
    turned = turn_call(queries)
    reverse = reversed_taps(medium_filter)
    gain = norm_gain.astype(f32)[None, :]
    a, b, given, tail, turned, reverse, gain = lax.optimization_barrier((a, b, given, tail, turned, reverse, gain))
    a_line, b_line = jnp.stack(a), jnp.stack(b)
    lines = [moved(a_line, y=1), moved(a_line, y=-1), moved(b_line, z=1), moved(b_line, z=-1)]
    turned = [turned, turn_call(given)]
    states = attend_call(near, [part[None] for part in a + b], turned, [None, None])
    a_line, b_line, tail, states = lax.optimization_barrier((a_line, b_line, tail, states))
    crossed = [moved(a_line, y=2), moved(b_line, z=2)]
    halo = lax.ppermute(tail, "ctx", [(i, i + 1) for i in range(BLOCKS - 1)])
    states = attend_call(far, lines, turned, states)
    kept, helped = attend_call(across, crossed, turned, states, last=True)
    returned = lax.ppermute(helped, "ctx", [(mirrored(i), i) for i in lenders])
    halo, helped = lax.optimization_barrier((halo, helped))
    branch, squares = mixer_call(stream_one, stream_two, stream_value, halo, short_stream_taps, reverse, residual)
    sums = squares
    sums, returned = lax.optimization_barrier((sums, returned))
    parts = [lax.ppermute(sums, "tp", [(i, i ^ step) for i in range(4)]) for step in (1, 2, 3)]
    least = [min(i for i in lenders if lent[i] > level) for level in range(LENT)]
    count = sum((me >= bound).astype(jnp.int32) for bound in least)
    bound = (OWN - count) * (UNIT * HD) - middle
    later = jnp.where(lax.broadcasted_iota(jnp.int32, returned.shape, 1) >= bound, returned, kept[:, middle:])
    attended = jnp.concatenate([kept[:, :middle], later], axis=1)
    scaling = lax.rsqrt((sums + parts[0] + parts[1] + parts[2]) / D + 1e-06)
    normed = (branch * scaling.reshape(rows, 1) * gain).astype(bf)
    return normed, attended


def solution(mesh):
    in_specs = (P("ctx", "tp"), P("ctx", "tp"), P("ctx", "tp"), P(None, None, "tp"), P("tp", None),
                P("ctx", "tp"), P("tp"), P("ctx", "tp"), P("ctx", "tp"), P("ctx", "tp"))
    return jax.shard_map(shards, mesh=mesh, in_specs=in_specs, out_specs=(P("ctx", "tp"), P("ctx", "tp")), check_vma=False)
```
